128 devices in a mesh: seq: 32 (over y, x, core), tp: 4 (over z).
Axes of the slice: x: 4, y: 4, z: 4, core: 2. Of those that a mesh axis runs over, the one named last changes fastest.
Arguments:
- projected: bfloat16 [18560, 32768], P(('tp', 'seq')), may hold values from -4 to 98
- conv_weight: float32 [4, 8, 1280], P(None, 'tp'), may hold values from -3 to 3
- dt_bias: float32 [128], P('tp'), may hold values from -7 to -1
- a_log: float32 [128], P('tp'), may hold values from -7 to -1
- d_skip: float32 [128], P('tp'), may hold values from 0.5 to 2
- norm_gain: float32 [8192], P('tp'), may hold values from 0.25 to 1.75
Outputs:
- mixer_out: bfloat16 [32768, 8192], P('seq', 'tp')
The draws below stay inside these ranges and needn't reach their ends.
All inputs are finite; a program needn't handle non-finite values.
Results may differ from the reference program's by a relative error of at most 0.0034.
Values may be sent and summed in bfloat16 or wider, within the bound.
A program may use at most 192 MiB of HBM per device.

```python
import math
import jax
import jax.numpy as jnp
from jax import lax

HEADS = 128
HEAD_DIM = 64
STATE_WIDTH = 128
GROUPS = 8
CONV_TAPS = 4
BLOCK = 256
TOK_DEV = 1024
CONVCH = 1280
INNER = 8192
PROMPT_TOKENS = 32768


def head_kinds(key, fast_share):
    return jax.random.uniform(key, (HEADS,)) < fast_share


def draw_projected(key, part):
    key = jax.random.fold_in(key, 7)
    random_splitkeys = jax.random.split(key, 4)
    heads_group = HEADS // GROUPS
    group_span_width = heads_group * HEAD_DIM
    group_cols = 2 * group_span_width + 2 * STATE_WIDTH + heads_group
    base_draw = jax.random.normal(random_splitkeys[0], (PROMPT_TOKENS, GROUPS, group_cols))
    base_draw = jnp.clip(base_draw, -4.0, 4.0)
    column_entry = jnp.arange(group_cols)
    column_scale = jnp.where(column_entry < 2 * group_span_width, 1.0, 0.5)
    value_rows = base_draw * column_scale[None, None, :]
    regions = PROMPT_TOKENS // TOK_DEV
    offsets = jax.random.uniform(random_splitkeys[2], (regions,), minval=-0.7, maxval=0.35)
    token_position = jnp.arange(PROMPT_TOKENS)
    segment_offset = offsets[token_position // TOK_DEV]
    spike_position = jax.random.randint(random_splitkeys[3], (2,), CONV_TAPS - 1, PROMPT_TOKENS)
    inside_spike = jnp.any(token_position[:, None] == spike_position[None, :], axis=1)
    beside_spike = jnp.any((token_position[:, None] <= spike_position[None, :]) & (token_position[:, None] >= spike_position[None, :] - (CONV_TAPS - 1)), axis=1)
    spike_height = math.floor(math.sqrt(PROMPT_TOKENS) / 2) + 8.0
    is_step = column_entry >= group_cols - heads_group
    carries_state = (column_entry >= group_span_width) & (column_entry < 2 * group_span_width + STATE_WIDTH)
    increment_values = jnp.where(inside_spike[:, None, None], spike_height, segment_offset[:, None, None] + value_rows)
    value_rows = jnp.where(is_step[None, None, :], increment_values, value_rows)
    value_rows = jnp.where(beside_spike[:, None, None] & carries_state[None, None, :], value_rows * 0.001, value_rows)
    return jnp.transpose(value_rows.reshape(PROMPT_TOKENS, GROUPS * group_cols)).astype(jnp.bfloat16)


def draw_dt_bias(key, part):
    fast_share = 0.5
    fast_heads = head_kinds(key, fast_share)
    key = jax.random.fold_in(key, 3)
    random_splitkeys = jax.random.split(key, 4)
    slow_bias = jnp.log(jax.random.uniform(random_splitkeys[0], (HEADS,), minval=0.5, maxval=1.0)) - 0.5 * math.log(PROMPT_TOKENS)
    short_bias = jax.random.uniform(random_splitkeys[1], (HEADS,), minval=-2.2, maxval=-1.4)
    small_bias = jax.random.uniform(random_splitkeys[3], (HEADS,), minval=-7.0, maxval=-6.0)
    small_steps = jax.random.uniform(random_splitkeys[2], (HEADS,)) < 0.5
    fast_bias = jnp.where(small_steps, small_bias, short_bias)
    return jnp.where(fast_heads, fast_bias, slow_bias).astype(jnp.float32)


def draw_a_log(key, part):
    fast_share = 0.5
    fast_heads = head_kinds(key, fast_share)
    key = jax.random.fold_in(key, 5)
    random_splitkeys = jax.random.split(key, 2)
    slow_rate = jnp.log(jax.random.uniform(random_splitkeys[0], (HEADS,), minval=0.5, maxval=1.0)) - 0.5 * math.log(PROMPT_TOKENS)
    fast_rate = jax.random.uniform(random_splitkeys[1], (HEADS,), minval=math.log(0.1), maxval=math.log(0.25))
    return jnp.where(fast_heads, fast_rate, slow_rate).astype(jnp.float32)


def levels(own_key, dims, shards, low, largest):
    factor_of, own = 1.0, jax.random.fold_in(own_key, 6)
    for dim, parts in shards:
        heights = jnp.exp(jax.random.uniform(jax.random.fold_in(own, dim), (parts,), jnp.float32, low / len(shards), largest / len(shards)))
        factor_of = factor_of * jnp.repeat(heights, dims[dim] // parts).reshape([-1 if axis == dim else 1 for axis in range(len(dims))])
    return factor_of


def bell_draw(rng, shape, width, most, cuts=(), dtype=jnp.bfloat16):
    level = levels(rng, shape, cuts, -0.22, 0.18) if cuts else 1.0
    entries = jax.random.normal(rng, shape, jnp.float32) * width * level
    return jnp.minimum(jnp.maximum(entries, -most), most).astype(dtype)


def setup_inputs(seed: int = 0) -> dict:
    key_of = jax.random.split(jax.random.key(seed), 7)
    return {
        "projected": draw_projected(jax.random.fold_in(key_of[6], 71), 0),
        "conv_weight": bell_draw(key_of[1], (CONV_TAPS, GROUPS, CONVCH), CONV_TAPS ** -0.5, 3.0, ((1, 4),), jnp.float32),
        "dt_bias": draw_dt_bias(jax.random.fold_in(key_of[6], 71), 0),
        "a_log": draw_a_log(jax.random.fold_in(key_of[6], 71), 0),
        "d_skip": jnp.clip(0.5 + 1.5 * jax.random.uniform(key_of[4], (HEADS,), jnp.float32) ** levels(key_of[4], (HEADS,), ((0, 4),), -0.2, 0.2), 0.5, 2.0),
        "norm_gain": jnp.clip(1.0 + 0.15 * jax.random.normal(key_of[5], (INNER,), jnp.float32), 0.25, 1.75),
    }


epsilon = 1e-05

def block_step(state_now, pieces):
    block_values, block_input, block_output, block_decay, block_steps = pieces
    f32 = jnp.float32
    running = jnp.cumsum(block_decay, axis=0)
    length = running.shape[0]
    scores = jnp.einsum('tgn,sgn->gts', block_output.astype(f32), block_input.astype(f32), precision=lax.Precision.HIGHEST)
    running_heads = jnp.transpose(running, (1, 2, 0))
    log_gaps = running_heads[:, :, :, None] - running_heads[:, :, None, :]
    row_index = lax.broadcasted_iota(jnp.int32, (length, length), 0)
    col_index = lax.broadcasted_iota(jnp.int32, (length, length), 1)
    decays = jnp.exp(jnp.where(row_index >= col_index, log_gaps, -jnp.inf))
    weights = (scores[:, None] * decays * jnp.transpose(block_steps, (1, 2, 0))[:, :, None, :]).astype(jnp.bfloat16)
    intra_part = jnp.einsum('gjts,sgjp->tgjp', weights.astype(f32), block_values.astype(f32), precision=lax.Precision.HIGHEST)
    carried = jnp.exp(running)[..., None] * jnp.einsum('tgn,gjpn->tgjp', block_output.astype(f32), state_now, precision=lax.Precision.HIGHEST)
    block_end = running[-1]
    carry_scale = jnp.exp(block_end[None] - running) * block_steps
    weighted = (block_values.astype(f32) * carry_scale[..., None]).astype(jnp.bfloat16)
    update = jnp.einsum('sgjp,sgn->gjpn', weighted.astype(f32), block_input.astype(f32), precision=lax.Precision.HIGHEST)
    advanced = jnp.exp(block_end)[..., None, None] * state_now + update
    return (advanced, intra_part + carried)

def reference(projected, conv_weight, dt_bias, a_log, d_skip, norm_gain):
    f32 = jnp.float32
    token_count = projected.shape[1]
    heads_group = HEADS // GROUPS
    group_span_width = heads_group * HEAD_DIM
    conv_channels = group_span_width + 2 * STATE_WIDTH
    columns = jnp.transpose(projected).reshape(token_count, GROUPS, -1)
    gate_part = columns[:, :, :group_span_width]
    conv_input = columns[:, :, group_span_width:group_span_width + conv_channels].astype(f32)
    step_raw = columns[:, :, group_span_width + conv_channels:].astype(f32)
    padded = jnp.concatenate([jnp.zeros((CONV_TAPS - 1, GROUPS, conv_channels), f32), conv_input], axis=0)
    summed = conv_weight[0] * padded[0:token_count]
    for tap_index in range(1, CONV_TAPS):
        summed = summed + conv_weight[tap_index] * padded[tap_index:tap_index + token_count]
    activated = jax.nn.silu(summed).astype(jnp.bfloat16)
    head_values = activated[:, :, :group_span_width].reshape(token_count, GROUPS, heads_group, HEAD_DIM)
    input_map = activated[:, :, group_span_width:group_span_width + STATE_WIDTH]
    output_map = activated[:, :, group_span_width + STATE_WIDTH:]
    step_size = jax.nn.softplus(step_raw + dt_bias.reshape(GROUPS, heads_group))
    log_decay = -jnp.exp(a_log).reshape(GROUPS, heads_group) * step_size
    block_count = token_count // BLOCK

    def to_blocks(tensor):
        return tensor.reshape((block_count, BLOCK) + tensor.shape[1:])
    zero_state = jnp.zeros((GROUPS, heads_group, HEAD_DIM, STATE_WIDTH), f32)
    _, block_outputs = lax.scan(block_step, zero_state, (to_blocks(head_values), to_blocks(input_map), to_blocks(output_map), to_blocks(log_decay), to_blocks(step_size)))
    mixed_out = block_outputs.reshape(token_count, GROUPS, heads_group, HEAD_DIM) + d_skip.reshape(GROUPS, heads_group)[:, :, None] * head_values.astype(f32)
    gated_out = mixed_out.reshape(token_count, GROUPS, group_span_width) * jax.nn.silu(gate_part.astype(f32))
    mean_square = lax.optimization_barrier(jnp.mean(gated_out * gated_out, axis=-1, keepdims=True))
    normed = gated_out * lax.rsqrt(mean_square + epsilon) * norm_gain.reshape(GROUPS, group_span_width)
    return normed.reshape(token_count, GROUPS * group_span_width).astype(jnp.bfloat16)
```

```python
import jax
import jax.numpy as jnp
from jax import lax
from jax.sharding import PartitionSpec as P

HEAD_DIM = 64
STATE_WIDTH = 128
BLOCK = 256


epsilon = 1e-05


def passed_along(shard, axis, by):
    count = lax.axis_size(axis)
    pairs = [(i, i + by) for i in range(count) if 0 <= i + by < count]
    return lax.ppermute(shard, axis, pairs)


def block_step(state_now, pieces):
    block_values, block_input, block_output, block_decay, block_steps = pieces
    running = jnp.cumsum(block_decay, axis=0)
    length = running.shape[0]
    scores = jnp.einsum(
        "tgn,sgn->gts", block_output, block_input, preferred_element_type=jnp.float32
    )
    running_heads = jnp.transpose(running, (1, 2, 0))
    log_gaps = running_heads[:, :, :, None] - running_heads[:, :, None, :]
    row_index = lax.broadcasted_iota(jnp.int32, (length, length), 0)
    col_index = lax.broadcasted_iota(jnp.int32, (length, length), 1)
    decays = jnp.exp(jnp.where(row_index >= col_index, log_gaps, -jnp.inf))
    weights = (
        scores[:, None] * decays * jnp.transpose(block_steps, (1, 2, 0))[:, :, None, :]
    ).astype(jnp.bfloat16)
    intra_part = jnp.einsum(
        "gjts,sgjp->tgjp", weights, block_values, preferred_element_type=jnp.float32
    )
    block_end = running[-1]
    carry_scale = jnp.exp(block_end[None] - running) * block_steps
    weighted = (block_values * carry_scale[..., None]).astype(jnp.bfloat16)
    update = jnp.einsum("sgjp,sgn->gjpn", weighted, block_input, preferred_element_type=jnp.float32)
    advanced = jnp.exp(block_end)[..., None, None] * state_now + update
    return (advanced, (state_now, intra_part, running))


def per_device(projected, conv_weight, dt_bias, a_log, d_skip, norm_gain):
    seq_count = lax.axis_size("seq")
    tap_count = conv_weight.shape[0]
    group_count = conv_weight.shape[1]
    conv_channels = conv_weight.shape[2]
    head_count = dt_bias.shape[0]
    heads_group = head_count // group_count
    group_span_width = heads_group * HEAD_DIM
    group_cols = 2 * group_span_width + 2 * STATE_WIDTH + heads_group
    slice_width, all_tokens = projected.shape
    local_tokens = all_tokens // seq_count
    received_rows = lax.all_to_all(projected, "seq", split_axis=1, concat_axis=0, tiled=True)
    columns = jnp.transpose(received_rows).reshape(local_tokens, group_count, group_cols)
    conv_input = columns[:, :, group_span_width : group_span_width + conv_channels]
    rim_rows = passed_along(conv_input[local_tokens - (tap_count - 1) :], "seq", 1)
    padded = jnp.concatenate([rim_rows, conv_input], axis=0)
    summed = conv_weight[0] * padded[0:local_tokens]
    for tap_index in range(1, tap_count):
        summed = summed + conv_weight[tap_index] * padded[tap_index : tap_index + local_tokens]
    activated = jax.nn.silu(summed).astype(jnp.bfloat16)
    gate_part = columns[:, :, :group_span_width]
    step_raw = columns[:, :, group_span_width + conv_channels :].astype(jnp.float32)
    head_values = activated[:, :, :group_span_width].reshape(
        local_tokens, group_count, heads_group, HEAD_DIM
    )
    input_map = activated[:, :, group_span_width : group_span_width + STATE_WIDTH]
    output_map = activated[:, :, group_span_width + STATE_WIDTH :]
    step_size = jax.nn.softplus(step_raw + dt_bias.reshape(group_count, heads_group))
    log_decay = -jnp.exp(a_log).reshape(group_count, heads_group) * step_size
    block_count = local_tokens // BLOCK

    def to_blocks(tensor):
        return tensor.reshape((block_count, BLOCK) + tensor.shape[1:])

    zero_state = jnp.zeros((group_count, heads_group, HEAD_DIM, STATE_WIDTH), jnp.float32)
    device_state, (block_states, intra_parts, running) = lax.scan(
        block_step,
        zero_state,
        (
            to_blocks(head_values),
            to_blocks(input_map),
            to_blocks(output_map),
            to_blocks(log_decay),
            to_blocks(step_size),
        ),
    )
    block_ends = running[:, -1]
    lead_in = jnp.cumsum(block_ends, axis=0) - block_ends

    device_log = jnp.sum(block_ends, axis=0).reshape(head_count)
    sent = device_state.reshape(head_count, HEAD_DIM * STATE_WIDTH)
    owned = lax.all_to_all(sent, "seq", split_axis=0, concat_axis=0, tiled=True)
    logs = lax.all_to_all(device_log, "seq", split_axis=0, concat_axis=0, tiled=True)
    to_device = lax.broadcasted_iota(jnp.int32, (seq_count, seq_count, seq_count), 0)
    from_device = lax.broadcasted_iota(jnp.int32, (seq_count, seq_count, seq_count), 1)
    between = lax.broadcasted_iota(jnp.int32, (seq_count, seq_count, seq_count), 2)
    inside = (between > from_device) & (between < to_device)
    span_log = jnp.sum(jnp.where(inside, logs[None, None, :], 0.0), axis=-1)
    span = jnp.where(from_device[:, :, 0] < to_device[:, :, 0], jnp.exp(span_log), 0.0)
    arrived = jnp.dot(span, owned, precision=lax.Precision.HIGHEST)
    incoming = lax.all_to_all(arrived, "seq", split_axis=0, concat_axis=0, tiled=True)
    incoming = incoming.reshape(zero_state.shape)
    full_states = block_states + jnp.exp(lead_in)[..., None, None] * incoming[None]
    carried_part = jnp.exp(running)[..., None] * jnp.einsum(
        "ktgn,kgjpn->ktgjp",
        to_blocks(output_map).astype(jnp.float32),
        full_states,
        precision=lax.Precision.HIGHEST,
    )
    mixed_out = (intra_parts + carried_part).reshape(
        local_tokens, group_count, heads_group, HEAD_DIM
    ) + d_skip.reshape(group_count, heads_group)[:, :, None] * head_values.astype(jnp.float32)
    gated_out = mixed_out.reshape(local_tokens, group_count, group_span_width) * jax.nn.silu(
        gate_part.astype(jnp.float32)
    )
    mean_square = jnp.mean(gated_out * gated_out, axis=-1, keepdims=True)
    normed = (
        gated_out
        * lax.rsqrt(mean_square + epsilon)
        * norm_gain.reshape(group_count, group_span_width)
    )
    return normed.reshape(local_tokens, group_count * group_span_width).astype(jnp.bfloat16)


def solution(mesh):
    in_specs = (P(("tp", "seq"), None), P(None, "tp", None), P("tp"), P("tp"), P("tp"), P("tp"))
    out_specs = P("seq", "tp")
    return jax.shard_map(
        per_device, mesh=mesh, in_specs=in_specs, out_specs=out_specs, check_vma=False
    )
```

```python
import functools

import jax
import jax.numpy as jnp
from jax import lax
from jax.experimental import pallas as pl
from jax.experimental.pallas import tpu as pltpu
from jax.sharding import PartitionSpec as P

MESH = pl.DeviceIdType.MESH
HEAD_DIM = 64
STATE_WIDTH = 128
CHUNK = 128
CHUNKS = 8
GROUPS = 2
HEADS = 16
SPAN = HEADS * HEAD_DIM
CONV = SPAN + 2 * STATE_WIDTH
COLS = SPAN + CONV + HEADS
EPSILON = 1e-05

F32 = jnp.float32
BF16 = jnp.bfloat16


def silu(v):
    return v * (1.0 / (1.0 + jnp.exp(-v)))


def dot(a, b, precision=None):
    return jnp.dot(a, b, preferred_element_type=F32, precision=precision)


def kernel(
    n, x_ref, conv_ref, par_ref, gain_ref, out_ref,
    recv, rows, taps, prev, act, wgt, state, ys, gate, outmap, reach, lead, bmat,
    halo_out, halo_in, own, gathered, prefix, incoming, fade_out, fade_in, staged,
    chunk_send, chunk_recv, chunk_own, halo_send, halo_recv,
    scan_send, scan_recv, fade_send, fade_recv, back_send, back_recv, out_sem,
):
    me = lax.axis_index("seq")
    slab = COLS * GROUPS // n
    per_group = n // GROUPS
    per_device = GROUPS * HEADS // n

    barrier = pltpu.get_barrier_semaphore()

    def greet(i, _):
        pl.semaphore_signal(
            barrier, inc=1, device_id={"seq": lax.rem(me + i, n)}, device_id_type=MESH
        )
        return 0

    lax.fori_loop(1, n, greet, 0)
    pl.semaphore_wait(barrier, n - 1)

    def piece(device, c):
        first = pl.multiple_of(device * (CHUNK * CHUNKS) + c * CHUNK, CHUNK)
        return x_ref.at[:, pl.ds(first, CHUNK)]

    def send_chunk(turn, _):
        c = lax.rem(turn + CHUNKS - 1, CHUNKS)
        pltpu.make_async_copy(piece(me, c), recv.at[c, me], chunk_own.at[c]).start()

        def send(i, _):
            device = lax.rem(me + i, n)
            pltpu.make_async_remote_copy(
                src_ref=piece(device, c),
                dst_ref=recv.at[c, me],
                send_sem=chunk_send.at[c],
                recv_sem=chunk_recv.at[c],
                device_id={"seq": device},
                device_id_type=MESH,
            ).start()
            return 0

        lax.fori_loop(1, n, send, 0)
        return 0

    lax.fori_loop(0, CHUNKS, send_chunk, 0)

    def wait_chunk(c):
        peers = recv.at[c, pl.ds(0, n - 1)]
        pltpu.make_async_copy(peers, peers, chunk_recv.at[c]).wait()
        pltpu.make_async_copy(recv.at[c, 0], recv.at[c, 0], chunk_own.at[c]).wait()

    sub = lax.broadcasted_iota(jnp.int32, (CHUNK, CHUNK), 0)
    lane = lax.broadcasted_iota(jnp.int32, (CHUNK, CHUNK), 1)
    causal = sub <= lane

    for g in range(GROUPS):
        for i in range(CONV // CHUNK):
            four = jnp.concatenate(
                [conv_ref[k, g : g + 1, i * CHUNK : (i + 1) * CHUNK] for k in range(4)]
                + [jnp.zeros((CHUNK - 4, CHUNK), F32)],
                axis=0,
            )
            turned = jnp.transpose(four)
            for k in range(4):
                taps[g, k, i * CHUNK : (i + 1) * CHUNK, :] = jnp.broadcast_to(
                    turned[:, k : k + 1], (CHUNK, CHUNK)
                )
    lead[...] = jnp.zeros_like(lead)
    state[...] = jnp.zeros_like(state)

    def lay_out(c, g):
        for k in range(per_group):
            rows[k * slab : (k + 1) * slab, :] = recv[c, g * per_group + k].astype(F32)

    wait_chunk(CHUNKS - 1)

    def make_halo(g, _):
        lay_out(CHUNKS - 1, g)
        for i in range(CONV // CHUNK):
            tile = rows[SPAN + i * CHUNK : SPAN + (i + 1) * CHUNK, :]
            halo_out[g, :, i * CHUNK : (i + 1) * CHUNK] = jnp.transpose(tile)[CHUNK - 8 :, :]
        return 0

    lax.fori_loop(0, GROUPS, make_halo, 0)
    halo_copy = pltpu.make_async_remote_copy(
        src_ref=halo_out,
        dst_ref=halo_in,
        send_sem=halo_send,
        recv_sem=halo_recv,
        device_id={"seq": lax.rem(me + 1, n)},
        device_id_type=MESH,
    )
    halo_copy.start()
    halo_copy.wait()
    has_past = jnp.where(me > 0, 1.0, 0.0).astype(F32)
    for g in range(GROUPS):
        for i in range(CONV // CHUNK):
            tail = halo_in[g, :, i * CHUNK : (i + 1) * CHUNK] * has_past
            tile = jnp.concatenate([jnp.zeros((CHUNK - 8, CHUNK), F32), tail], axis=0)
            prev[g, i * CHUNK : (i + 1) * CHUNK, :] = jnp.transpose(tile)

    def unit(u, _):
        c = u // GROUPS
        g = lax.rem(u, GROUPS)

        @pl.when(jnp.logical_and(g == 0, c < CHUNKS - 1))
        def _():
            wait_chunk(c)

        lay_out(c, g)
        for i in range(SPAN // CHUNK):
            gate[u, i * CHUNK : (i + 1) * CHUNK, :] = silu(rows[i * CHUNK : (i + 1) * CHUNK, :])
        for i in range(CONV // CHUNK):
            span = slice(i * CHUNK, (i + 1) * CHUNK)
            current = rows[SPAN + i * CHUNK : SPAN + (i + 1) * CHUNK, :]
            past = prev[g, span, :]
            total = taps[g, 3, span, :] * current
            for k in range(1, 4):
                shifted = pltpu.roll(jnp.where(lane >= CHUNK - k, past, current), k, 1)
                total += taps[g, 3 - k, span, :] * shifted
            prev[g, span, :] = current
            value = silu(total)
            if i < SPAN // CHUNK:
                act[span, :] = value.astype(BF16)
            elif i == SPAN // CHUNK:
                bmat[...] = jnp.transpose(value).astype(BF16)
            else:
                outmap[u] = value.astype(BF16)

        raw = rows[SPAN + CONV :, :] + par_ref[0, g]
        step = jnp.maximum(raw, 0.0) + jnp.log1p(jnp.exp(-jnp.abs(raw)))
        log_decay = -jnp.exp(par_ref[1, g]) * step
        running = dot(log_decay, causal.astype(F32), lax.Precision.HIGHEST)
        last = jnp.broadcast_to(running[:, CHUNK - 1 :], (HEADS, CHUNK))
        since = jnp.exp(running)
        until = jnp.exp(last - running) * step
        fade = jnp.exp(last)
        reach[u] = jnp.exp(running + lead[g])
        lead[g] += last
        columns = jnp.transpose(
            jnp.concatenate(
                [running - jnp.log(step), jnp.zeros((CHUNK - HEADS, CHUNK), F32)], axis=0
            )
        )
        cmat = outmap[u]
        scores = dot(bmat[...], cmat)
        high = state[g].astype(BF16)
        low = (state[g] - high.astype(F32)).astype(BF16)
        carried = dot(
            jnp.concatenate([high, low], axis=1), jnp.concatenate([cmat, cmat], axis=0)
        )
        ys[u] = carried
        for h in range(HEADS):
            span = slice(h * HEAD_DIM, (h + 1) * HEAD_DIM)
            gaps = running[h : h + 1, :] - columns[:, h : h + 1]
            weights = (scores * jnp.exp(jnp.where(causal, gaps, -jnp.inf))).astype(BF16)
            x = act[span, :]
            wide = x.astype(F32)
            ys[u, span, :] = (
                dot(x, weights)
                + par_ref[2, g, h : h + 1, :] * wide
                + ys[u, span, :] * since[h : h + 1, :]
            )
            wgt[span, :] = (wide * until[h : h + 1, :]).astype(BF16)
        update = dot(wgt[...], bmat[...])
        for h in range(HEADS):
            span = slice(h * HEAD_DIM, (h + 1) * HEAD_DIM)
            state[g, span, :] = state[g, span, :] * fade[h : h + 1, :] + update[span, :]
        return 0

    lax.fori_loop(0, CHUNKS * GROUPS, unit, 0)

    for g in range(GROUPS):
        own[g * SPAN : (g + 1) * SPAN, :] = state[g].astype(BF16)
        for h in range(HEADS):
            first = (g * HEADS + h) * 8
            fade_out[first : first + 8, :] = jnp.broadcast_to(
                jnp.exp(lead[g, h : h + 1, :]), (8, CHUNK)
            )

    def heads_of(ref, device, height):
        size = per_device * height
        return ref.at[pl.ds(pl.multiple_of(device * size, size), size)]

    def send_states(i, _):
        device = lax.rem(me + i, n)
        for source, target, send_sem, recv_sem, height in (
            (own, gathered, scan_send, scan_recv, HEAD_DIM),
            (fade_out, fade_in, fade_send, fade_recv, 8),
        ):
            pltpu.make_async_remote_copy(
                src_ref=heads_of(source, device, height),
                dst_ref=heads_of(target, me, height),
                send_sem=send_sem,
                recv_sem=recv_sem,
                device_id={"seq": device},
                device_id_type=MESH,
            ).start()
        return 0

    lax.fori_loop(1, n, send_states, 0)
    heads_of(gathered, me, HEAD_DIM)[...] = heads_of(own, me, HEAD_DIM)[...]
    heads_of(fade_in, me, 8)[...] = heads_of(fade_out, me, 8)[...]

    def wait_all(ref, sem, height):
        peers = ref.at[pl.ds(0, (n - 1) * per_device * height)]
        pltpu.make_async_copy(peers, peers, sem).wait()

    wait_all(gathered, scan_recv, HEAD_DIM)
    wait_all(fade_in, fade_recv, 8)

    def horner(device, reached):
        heads_of(prefix, device, HEAD_DIM)[...] = reached.reshape(
            per_device * HEAD_DIM, STATE_WIDTH
        ).astype(BF16)
        factor = heads_of(fade_in, device, 8)[...].reshape(per_device, 1, 8, STATE_WIDTH)
        added = heads_of(gathered, device, HEAD_DIM)[...].astype(F32)
        return reached * factor + added.reshape(per_device, 8, 8, STATE_WIDTH)

    lax.fori_loop(0, n, horner, jnp.zeros((per_device, 8, 8, STATE_WIDTH), F32))

    def send_back(i, _):
        device = lax.rem(me + i, n)
        pltpu.make_async_remote_copy(
            src_ref=heads_of(prefix, device, HEAD_DIM),
            dst_ref=heads_of(incoming, me, HEAD_DIM),
            send_sem=back_send,
            recv_sem=back_recv,
            device_id={"seq": device},
            device_id_type=MESH,
        ).start()
        return 0

    lax.fori_loop(1, n, send_back, 0)
    heads_of(incoming, me, HEAD_DIM)[...] = heads_of(prefix, me, HEAD_DIM)[...]
    wait_all(incoming, back_recv, HEAD_DIM)

    def finish(u, _):
        c = u // GROUPS
        g = lax.rem(u, GROUPS)
        arrived = dot(
            incoming[pl.ds(pl.multiple_of(g * SPAN, SPAN), SPAN), :], outmap[u]
        )
        squares = jnp.zeros((1, CHUNK), F32)
        for h in range(HEADS):
            span = slice(h * HEAD_DIM, (h + 1) * HEAD_DIM)
            mixed = ys[u, span, :] + arrived[span, :] * reach[u, h : h + 1, :]
            gated = mixed * gate[u, span, :]
            ys[u, span, :] = gated
            squares += jnp.sum(gated * gated, axis=0, keepdims=True)
        scale = lax.rsqrt(squares * (1.0 / SPAN) + EPSILON)
        for i in range(SPAN // CHUNK):
            span = slice(i * CHUNK, (i + 1) * CHUNK)
            turned = jnp.transpose(ys[u, span, :] * scale)
            staged[u, :, span] = (turned * gain_ref[g, :, span]).astype(BF16)
        pltpu.make_async_copy(
            staged.at[u],
            out_ref.at[
                pl.ds(pl.multiple_of(c * CHUNK, CHUNK), CHUNK),
                pl.ds(pl.multiple_of(g * SPAN, SPAN), SPAN),
            ],
            out_sem,
        ).start()
        return 0

    lax.fori_loop(0, CHUNKS * GROUPS, finish, 0)

    def drain(c, _):
        peers = recv.at[c, pl.ds(0, n - 1)]
        pltpu.make_async_copy(peers, peers, chunk_send.at[c]).wait()
        return 0

    lax.fori_loop(0, CHUNKS, drain, 0)
    wait_all(own, scan_send, HEAD_DIM)
    wait_all(fade_out, fade_send, 8)
    wait_all(prefix, back_send, HEAD_DIM)
    pltpu.make_async_copy(staged, staged, out_sem).wait()


def per_device(projected, conv_weight, dt_bias, a_log, d_skip, norm_gain):
    n = lax.axis_size("seq")
    slab = COLS * GROUPS // n
    tokens = CHUNK * CHUNKS
    units = GROUPS * CHUNKS
    heads = GROUPS * HEADS
    params = jnp.broadcast_to(
        jnp.stack([dt_bias, a_log, d_skip]).reshape(3, GROUPS, HEADS, 1),
        (3, GROUPS, HEADS, CHUNK),
    )
    gain = norm_gain.reshape(GROUPS, 1, SPAN)
    vmem = pl.BlockSpec(memory_space=pltpu.VMEM)
    anywhere = pl.BlockSpec(memory_space=pl.ANY)
    dma = pltpu.SemaphoreType.DMA
    return pl.pallas_call(
        functools.partial(kernel, n),
        out_shape=jax.ShapeDtypeStruct((tokens, GROUPS * SPAN), BF16),
        in_specs=[anywhere, vmem, vmem, vmem],
        out_specs=anywhere,
        scratch_shapes=[
            pltpu.VMEM((CHUNKS, n, slab, CHUNK), BF16),
            pltpu.VMEM((COLS, CHUNK), F32),
            pltpu.VMEM((GROUPS, 4, CONV, CHUNK), F32),
            pltpu.VMEM((GROUPS, CONV, CHUNK), F32),
            pltpu.VMEM((SPAN, CHUNK), BF16),
            pltpu.VMEM((SPAN, CHUNK), BF16),
            pltpu.VMEM((GROUPS, SPAN, STATE_WIDTH), F32),
            pltpu.VMEM((units, SPAN, CHUNK), F32),
            pltpu.VMEM((units, SPAN, CHUNK), F32),
            pltpu.VMEM((units, STATE_WIDTH, CHUNK), BF16),
            pltpu.VMEM((units, HEADS, CHUNK), F32),
            pltpu.VMEM((GROUPS, HEADS, CHUNK), F32),
            pltpu.VMEM((CHUNK, STATE_WIDTH), BF16),
            pltpu.VMEM((GROUPS, 8, CONV), F32),
            pltpu.VMEM((GROUPS, 8, CONV), F32),
            pltpu.VMEM((heads * HEAD_DIM, STATE_WIDTH), BF16),
            pltpu.VMEM((heads * HEAD_DIM, STATE_WIDTH), BF16),
            pltpu.VMEM((heads * HEAD_DIM, STATE_WIDTH), BF16),
            pltpu.VMEM((heads * HEAD_DIM, STATE_WIDTH), BF16),
            pltpu.VMEM((heads * 8, STATE_WIDTH), F32),
            pltpu.VMEM((heads * 8, STATE_WIDTH), F32),
            pltpu.VMEM((units, CHUNK, SPAN), BF16),
            dma((CHUNKS,)), dma((CHUNKS,)), dma((CHUNKS,)), dma, dma,
            dma, dma, dma, dma, dma, dma, dma,
        ],
        compiler_params=pltpu.CompilerParams(
            collective_id=0, has_side_effects=True, vmem_limit_bytes=58 * 2**20
        ),
    )(projected, conv_weight, params, gain)


def solution(mesh):
    in_specs = (P(("tp", "seq"), None), P(None, "tp", None), P("tp"), P("tp"), P("tp"), P("tp"))
    return jax.shard_map(
        per_device, mesh=mesh, in_specs=in_specs, out_specs=P("seq", "tp"), check_vma=False
    )
```

```python
import functools

import jax
import jax.numpy as jnp
from jax import lax
from jax.experimental import pallas as pl
from jax.experimental.pallas import tpu as pltpu
from jax.sharding import PartitionSpec as P

MESH = pl.DeviceIdType.MESH
HEAD_DIM = 64
STATE_WIDTH = 128
CHUNK = 128
CHUNKS = 8
GROUPS = 2
HEADS = 16
SPAN = HEADS * HEAD_DIM
CONV = SPAN + 2 * STATE_WIDTH
COLS = SPAN + CONV + HEADS
EPSILON = 1e-05
AHEAD = 3
HELD = 4
MESSAGE = HEAD_DIM + 16

F32 = jnp.float32
BF16 = jnp.bfloat16


def silu(v):
    return v * (1.0 / (1.0 + jnp.exp(-v)))


def dot(a, b, precision=None):
    return jnp.dot(a, b, preferred_element_type=F32, precision=precision)


def dot_nt(a, b):
    return lax.dot_general(a, b, (((1,), (1,)), ((), ())), preferred_element_type=F32)


def kernel(
    n, x_ref, conv_hbm, bias_hbm, rate_hbm, skip_hbm, gain_hbm, out_ref,
    conv_ref, bias_ref, rate_ref, skip_ref, gain_ref, recv, rows, gates, taps, params, prev, act, wgt, state, carried, within, into,
    outmap, outrows, small, lead, turned_gate, turned_own,
    halo_out, halo_in, own, gathered, prefix, incoming, staged,
    chunk_send, chunk_recv, chunk_own, halo_send, halo_recv,
    scan_send, scan_recv, back_send, back_recv, out_sem, small_sem,
):
    me = lax.axis_index("seq")
    slab = COLS * GROUPS // n
    per_group = n // GROUPS
    per_device = GROUPS * HEADS // n

    loads = [
        pltpu.make_async_copy(source, target, small_sem.at[k])
        for k, (source, target) in enumerate(
            (
                (conv_hbm, conv_ref),
                (bias_hbm, bias_ref),
                (rate_hbm, rate_ref),
                (skip_hbm, skip_ref),
                (gain_hbm, gain_ref),
            )
        )
    ]
    for load in loads:
        load.start()

    barrier = pltpu.get_barrier_semaphore()

    def greet(i, _):
        pl.semaphore_signal(
            barrier, inc=1, device_id={"seq": lax.rem(me + i, n)}, device_id_type=MESH
        )
        return 0

    lax.fori_loop(1, n, greet, 0)
    pl.semaphore_wait(barrier, n - 1)

    def peer(i, shift):
        move = lax.rem(i * 11 + shift, n - 1) + 1
        if n != 32:
            return lax.rem(me + move, n)
        y = lax.rem(me // 8 + move // 8, 4)
        x = lax.rem(me // 2 + move // 2, 4)
        core = lax.rem(me + move, 2)
        return y * 8 + x * 2 + core

    def piece(device, c):
        first = pl.multiple_of(device * (CHUNK * CHUNKS) + c * CHUNK, CHUNK)
        return x_ref.at[:, pl.ds(first, CHUNK)]

    def send_chunk(turn, _):
        c = lax.rem(turn + CHUNKS - 1, CHUNKS)

        def send(i, _):
            device = peer(i, c * 5)
            pltpu.make_async_remote_copy(
                src_ref=piece(device, c),
                dst_ref=recv.at[c, me],
                send_sem=chunk_send.at[c],
                recv_sem=chunk_recv.at[c],
                device_id={"seq": device},
                device_id_type=MESH,
            ).start()
            return 0

        lax.fori_loop(0, n - 1, send, 0)
        pltpu.make_async_copy(piece(me, c), recv.at[c, me], chunk_own.at[c]).start()
        return 0

    lax.fori_loop(0, AHEAD, send_chunk, 0)

    def wait_chunk(c):
        peers = recv.at[c, pl.ds(0, n - 1)]
        pltpu.make_async_copy(peers, peers, chunk_recv.at[c]).wait()
        pltpu.make_async_copy(recv.at[c, 0], recv.at[c, 0], chunk_own.at[c]).wait()

    sub = lax.broadcasted_iota(jnp.int32, (CHUNK, CHUNK), 0)
    lane = lax.broadcasted_iota(jnp.int32, (CHUNK, CHUNK), 1)
    causal = sub <= lane

    for load in loads:
        load.wait()

    def taps_of(g, i):
        four = jnp.concatenate(
            [conv_ref[k, g : g + 1, i * CHUNK : (i + 1) * CHUNK] for k in range(4)]
            + [jnp.zeros((CHUNK - 4, CHUNK), F32)],
            axis=0,
        )
        turned = jnp.transpose(four)
        for k in range(4):
            taps[g, k, i * CHUNK : (i + 1) * CHUNK, :] = jnp.broadcast_to(
                turned[:, k : k + 1], (CHUNK, CHUNK)
            )

    for g in range(GROUPS):
        for i in range(CONV // CHUNK):
            taps_of(g, i)
    rows[0:CHUNK, :] = jnp.zeros((CHUNK, CHUNK), F32)
    for k, ref in enumerate((bias_ref, rate_ref, skip_ref)):
        rows[k : k + 1, 0 : GROUPS * HEADS] = ref[...]
    turned = jnp.transpose(rows[0:CHUNK, :])
    for k in range(3):
        for g in range(GROUPS):
            params[k, g] = jnp.broadcast_to(
                turned[g * HEADS : (g + 1) * HEADS, k : k + 1], (HEADS, CHUNK)
            )
    lead[...] = jnp.zeros_like(lead)
    state[...] = jnp.zeros_like(state)

    def lay_out(c, g):
        for k in range(SPAN // slab, per_group):
            rows[k * slab : (k + 1) * slab, :] = recv[c, g * per_group + k].astype(F32)

    def lay_out_gates(c, g):
        for k in range(-(-SPAN // slab)):
            gates[k * slab : (k + 1) * slab, :] = recv[c, g * per_group + k].astype(F32)

    wait_chunk(CHUNKS - 1)
    send_chunk(AHEAD, 0)

    def make_halo(g, _):
        lay_out(CHUNKS - 1, g)
        for i in range(CONV // CHUNK):
            tile = rows[SPAN + i * CHUNK : SPAN + (i + 1) * CHUNK, :]
            halo_out[g, :, i * CHUNK : (i + 1) * CHUNK] = jnp.transpose(tile)[CHUNK - 8 :, :]
        return 0

    lax.fori_loop(0, GROUPS, make_halo, 0)
    halo_copy = pltpu.make_async_remote_copy(
        src_ref=halo_out,
        dst_ref=halo_in,
        send_sem=halo_send,
        recv_sem=halo_recv,
        device_id={"seq": lax.rem(me + 1, n)},
        device_id_type=MESH,
    )
    halo_copy.start()
    halo_copy.wait()
    has_past = jnp.where(me > 0, 1.0, 0.0).astype(F32)
    for g in range(GROUPS):
        for i in range(CONV // CHUNK):
            tail = halo_in[g, :, i * CHUNK : (i + 1) * CHUNK] * has_past
            tile = jnp.concatenate([jnp.zeros((CHUNK - 8, CHUNK), F32), tail], axis=0)
            prev[g, i * CHUNK : (i + 1) * CHUNK, :] = jnp.transpose(tile)

    def advance(u, _):
        c = u // GROUPS
        g = lax.rem(u, GROUPS)
        slot = lax.rem(u, HELD)

        @pl.when(jnp.logical_and(g == 0, c < CHUNKS - 1))
        def _():
            wait_chunk(c)

            @pl.when(c + 1 + AHEAD < CHUNKS)
            def _():
                send_chunk(c + 1 + AHEAD, 0)

        lay_out(c, g)
        for i in range(CONV // CHUNK):
            span = slice(i * CHUNK, (i + 1) * CHUNK)
            current = rows[SPAN + i * CHUNK : SPAN + (i + 1) * CHUNK, :]
            past = prev[g, span, :]
            total = taps[g, 3, span, :] * current
            for k in range(1, 4):
                shifted = pltpu.roll(jnp.where(lane >= CHUNK - k, past, current), k, 1)
                total += taps[g, 3 - k, span, :] * shifted
            prev[g, span, :] = current
            value = silu(total)
            if i < SPAN // CHUNK:
                act[slot, span, :] = value.astype(BF16)
            elif i == SPAN // CHUNK:
                into[slot] = jnp.transpose(value).astype(BF16)
            else:
                outmap[slot] = value.astype(BF16)
                outrows[u] = jnp.transpose(value).astype(BF16)

        raw = rows[SPAN + CONV : COLS, :] + params[0, g]
        step = jnp.maximum(raw, 0.0) + jnp.log1p(jnp.exp(-jnp.abs(raw)))
        log_decay = -jnp.exp(params[1, g]) * step
        running = dot(log_decay, causal.astype(F32), lax.Precision.HIGHEST)
        last = jnp.broadcast_to(running[:, CHUNK - 1 :], (HEADS, CHUNK))
        until = jnp.exp(last - running) * step
        fade = jnp.exp(last)
        small[slot, 0] = running
        small[slot, 1] = jnp.exp(running)
        small[slot, 2] = jnp.exp(running + lead[g])
        lead[g] += last
        within[slot] = jnp.transpose(
            jnp.concatenate(
                [running - jnp.log(step), jnp.zeros((CHUNK - HEADS, CHUNK), F32)], axis=0
            )
        )
        cmat = outmap[slot]
        high = state[g].astype(BF16)
        low = (state[g] - high.astype(F32)).astype(BF16)
        carried[slot] = dot(
            jnp.concatenate([high, low], axis=1), jnp.concatenate([cmat, cmat], axis=0)
        )
        for h in range(HEADS):
            span = slice(h * HEAD_DIM, (h + 1) * HEAD_DIM)
            wgt[span, :] = (act[slot, span, :].astype(F32) * until[h : h + 1, :]).astype(BF16)
        update = dot(wgt[...], into[slot])
        for h in range(HEADS):
            span = slice(h * HEAD_DIM, (h + 1) * HEAD_DIM)
            state[g, span, :] = state[g, span, :] * fade[h : h + 1, :] + update[span, :]
        return 0

    def mix(u, _):
        c = u // GROUPS
        g = lax.rem(u, GROUPS)
        slot = lax.rem(u, HELD)
        lay_out_gates(c, g)
        scores = dot(into[slot], outmap[slot])
        columns = within[slot]
        for pair in range(HEADS // 2):
            owns = []
            reaches = []
            for h in (2 * pair, 2 * pair + 1):
                span = slice(h * HEAD_DIM, (h + 1) * HEAD_DIM)
                gaps = small[slot, 0, h : h + 1, :] - columns[:, h : h + 1]
                weights = (scores * jnp.exp(jnp.where(causal, gaps, -jnp.inf))).astype(BF16)
                x = act[slot, span, :]
                mixed = (
                    dot(x, weights)
                    + params[2, g, h : h + 1, :] * x.astype(F32)
                    + carried[slot, span, :] * small[slot, 1, h : h + 1, :]
                )
                gate = silu(gates[span, :])
                owns.append(mixed * gate)
                reaches.append(gate * small[slot, 2, h : h + 1, :])
            span = slice(pair * 2 * HEAD_DIM, (pair + 1) * 2 * HEAD_DIM)
            turned_own[u, :, span] = jnp.transpose(jnp.concatenate(owns, axis=0))
            turned_gate[u, :, span] = jnp.transpose(jnp.concatenate(reaches, axis=0))
        return 0

    def unit(u, _):
        advance(u, 0)
        mix(u, 0)
        return 0

    units = CHUNKS * GROUPS
    lax.fori_loop(0, units - HELD, unit, 0)
    lax.fori_loop(units - HELD, units, advance, 0)

    low_sub = lax.broadcasted_iota(jnp.int32, (16, CHUNK), 0)
    for g in range(GROUPS):
        for h in range(HEADS):
            first = (g * HEADS + h) * MESSAGE
            own[first : first + HEAD_DIM, :] = state[
                g, h * HEAD_DIM : (h + 1) * HEAD_DIM, :
            ].astype(BF16)
            fade = jnp.broadcast_to(jnp.exp(lead[g, h : h + 1, :]), (16, CHUNK))
            high = fade.astype(BF16).astype(F32)
            middle = (fade - high).astype(BF16).astype(F32)
            parts = jnp.where(
                low_sub == 0,
                high,
                jnp.where(
                    low_sub == 1, middle, jnp.where(low_sub == 2, fade - high - middle, 0.0)
                ),
            )
            own[first + HEAD_DIM : first + MESSAGE, :] = parts.astype(BF16)

    def heads_of(ref, device, height):
        size = per_device * height
        return ref.at[pl.ds(pl.multiple_of(device * size, size), size)]

    def wait_all(ref, sem, height):
        peers = ref.at[pl.ds(0, (n - 1) * per_device * height)]
        pltpu.make_async_copy(peers, peers, sem).wait()

    def send_heads(source, target, height, send_sem, recv_sem):
        def send(i, _):
            device = peer(i, 0)
            pltpu.make_async_remote_copy(
                src_ref=heads_of(source, device, height),
                dst_ref=heads_of(target, me, height),
                send_sem=send_sem,
                recv_sem=recv_sem,
                device_id={"seq": device},
                device_id_type=MESH,
            ).start()
            return 0

        lax.fori_loop(0, n - 1, send, 0)
        heads_of(target, me, height)[...] = heads_of(source, me, height)[...]

    send_heads(own, gathered, MESSAGE, scan_send, scan_recv)
    lax.fori_loop(units - HELD, units, mix, 0)
    wait_all(gathered, scan_recv, MESSAGE)

    def horner(device, reached):
        heads_of(prefix, device, HEAD_DIM)[...] = reached.astype(BF16)
        message = heads_of(gathered, device, MESSAGE)[...].astype(F32)
        terms = []
        for h in range(per_device):
            first = h * MESSAGE
            fade = jnp.sum(message[first + HEAD_DIM : first + MESSAGE, :], axis=0, keepdims=True)
            terms.append(
                reached[h * HEAD_DIM : (h + 1) * HEAD_DIM, :] * fade
                + message[first : first + HEAD_DIM, :]
            )
        return terms[0] if per_device == 1 else jnp.concatenate(terms, axis=0)

    lax.fori_loop(0, n, horner, jnp.zeros((per_device * HEAD_DIM, STATE_WIDTH), F32))
    send_heads(prefix, incoming, HEAD_DIM, back_send, back_recv)
    wait_all(incoming, back_recv, HEAD_DIM)

    def finish(u, _):
        c = u // GROUPS
        g = lax.rem(u, GROUPS)
        arrived = dot_nt(
            outrows[u], incoming[pl.ds(pl.multiple_of(g * SPAN, SPAN), SPAN), :]
        )
        for i in range(CHUNK // 16):
            span = slice(i * 16, (i + 1) * 16)
            gated = turned_own[u, span, :] + arrived[span, :] * turned_gate[u, span, :]
            squares = jnp.sum(gated * gated, axis=1, keepdims=True)
            scale = lax.rsqrt(squares * (1.0 / SPAN) + EPSILON)
            staged[u, span, :] = (gated * scale * gain_ref[g]).astype(BF16)
        pltpu.make_async_copy(
            staged.at[u],
            out_ref.at[
                pl.ds(pl.multiple_of(c * CHUNK, CHUNK), CHUNK),
                pl.ds(pl.multiple_of(g * SPAN, SPAN), SPAN),
            ],
            out_sem,
        ).start()
        return 0

    lax.fori_loop(0, units, finish, 0)

    def drain(c, _):
        peers = recv.at[c, pl.ds(0, n - 1)]
        pltpu.make_async_copy(peers, peers, chunk_send.at[c]).wait()
        return 0

    lax.fori_loop(0, CHUNKS, drain, 0)
    wait_all(own, scan_send, MESSAGE)
    wait_all(prefix, back_send, HEAD_DIM)
    pltpu.make_async_copy(staged, staged, out_sem).wait()


def per_device(projected, conv_weight, dt_bias, a_log, d_skip, norm_gain):
    n = lax.axis_size("seq")
    slab = COLS * GROUPS // n
    tokens = CHUNK * CHUNKS
    units = GROUPS * CHUNKS
    heads = GROUPS * HEADS
    hbm = pl.BlockSpec(memory_space=pltpu.HBM)
    anywhere = pl.BlockSpec(memory_space=pl.ANY)
    dma = pltpu.SemaphoreType.DMA
    return pl.pallas_call(
        functools.partial(kernel, n),
        out_shape=jax.ShapeDtypeStruct((tokens, GROUPS * SPAN), BF16),
        in_specs=[hbm] * 6,
        out_specs=anywhere,
        scratch_shapes=[
            pltpu.VMEM((4, GROUPS, CONV), F32),
            pltpu.VMEM((1, heads), F32),
            pltpu.VMEM((1, heads), F32),
            pltpu.VMEM((1, heads), F32),
            pltpu.VMEM((GROUPS, 1, SPAN), F32),
            pltpu.VMEM((CHUNKS, n, slab, CHUNK), BF16),
            pltpu.VMEM((COLS, CHUNK), F32),
            pltpu.VMEM((-(-SPAN // slab) * slab, CHUNK), F32),
            pltpu.VMEM((GROUPS, 4, CONV, CHUNK), F32),
            pltpu.VMEM((3, GROUPS, HEADS, CHUNK), F32),
            pltpu.VMEM((GROUPS, CONV, CHUNK), F32),
            pltpu.VMEM((HELD, SPAN, CHUNK), BF16),
            pltpu.VMEM((SPAN, CHUNK), BF16),
            pltpu.VMEM((GROUPS, SPAN, STATE_WIDTH), F32),
            pltpu.VMEM((HELD, SPAN, CHUNK), F32),
            pltpu.VMEM((HELD, CHUNK, CHUNK), F32),
            pltpu.VMEM((HELD, CHUNK, STATE_WIDTH), BF16),
            pltpu.VMEM((HELD, STATE_WIDTH, CHUNK), BF16),
            pltpu.VMEM((units, CHUNK, STATE_WIDTH), BF16),
            pltpu.VMEM((HELD, 3, HEADS, CHUNK), F32),
            pltpu.VMEM((GROUPS, HEADS, CHUNK), F32),
            pltpu.VMEM((units, CHUNK, SPAN), F32),
            pltpu.VMEM((units, CHUNK, SPAN), F32),
            pltpu.VMEM((GROUPS, 8, CONV), F32),
            pltpu.VMEM((GROUPS, 8, CONV), F32),
            pltpu.VMEM((heads * MESSAGE, STATE_WIDTH), BF16),
            pltpu.VMEM((heads * MESSAGE, STATE_WIDTH), BF16),
            pltpu.VMEM((heads * HEAD_DIM, STATE_WIDTH), BF16),
            pltpu.VMEM((heads * HEAD_DIM, STATE_WIDTH), BF16),
            pltpu.VMEM((units, CHUNK, SPAN), BF16),
            dma((CHUNKS,)), dma((CHUNKS,)), dma((CHUNKS,)), dma, dma,
            dma, dma, dma, dma, dma, dma((5,)),
        ],
        compiler_params=pltpu.CompilerParams(
            collective_id=0, has_side_effects=True, vmem_limit_bytes=48 * 2**20
        ),
    )(
        projected, conv_weight,
        dt_bias.reshape(1, heads), a_log.reshape(1, heads), d_skip.reshape(1, heads),
        norm_gain.reshape(GROUPS, 1, SPAN),
    )


def solution(mesh):
    in_specs = (P(("tp", "seq"), None), P(None, "tp", None), P("tp"), P("tp"), P("tp"), P("tp"))
    return jax.shard_map(
        per_device, mesh=mesh, in_specs=in_specs, out_specs=P("seq", "tp"), check_vma=False
    )
```

```python
import functools

import jax
import jax.numpy as jnp
from jax import lax
from jax.experimental import pallas as pl
from jax.experimental.pallas import tpu as pltpu
from jax.sharding import PartitionSpec as P

MESH = pl.DeviceIdType.MESH
HEAD_DIM = 64
STATE_WIDTH = 128
CHUNK = 128
CHUNKS = 8
GROUPS = 2
HEADS = 16
SPAN = HEADS * HEAD_DIM
CONV = SPAN + 2 * STATE_WIDTH
COLS = SPAN + CONV + HEADS
EPSILON = 1e-05
AHEAD = 3
CONV_ROWS = 4 * GROUPS * CONV // CHUNK
HELD = 2
MESSAGE = HEAD_DIM + 16

F32 = jnp.float32
BF16 = jnp.bfloat16


def silu(v):
    return v * (1.0 / (1.0 + jnp.exp(-v)))


def dot(a, b, precision=None):
    return jnp.dot(a, b, preferred_element_type=F32, precision=precision)


def dot_nt(a, b):
    return lax.dot_general(a, b, (((1,), (1,)), ((), ())), preferred_element_type=F32)


def kernel(
    n, x_ref, pack_hbm, out_ref,
    pack_ref, recv, rows, gates, taps, params, prev, act, wgt, state, carried, within, into,
    outmap, outrows, small, lead, turned_gate, turned_own,
    tails, spare, extra_out, extra_in, extra, own, gathered, prefix, incoming, staged,
    chunk_send, chunk_recv, chunk_own, extra_send, extra_recv, tail_sem, spare_sem,
    scan_send, scan_recv, back_send, back_recv, out_sem, small_sem,
):
    me = lax.axis_index("seq")
    slab = COLS * GROUPS // n
    body = slab - 1
    per_group = n // GROUPS
    per_device = GROUPS * HEADS // n

    load = pltpu.make_async_copy(pack_hbm, pack_ref, small_sem)
    load.start()
    spare_load = pltpu.make_async_copy(x_ref.at[pl.ds(body, 1), :], spare, spare_sem)
    spare_load.start()

    def load_tail(device, _):
        first = pl.multiple_of((device + 1) * CHUNK * CHUNKS - CHUNK, CHUNK)
        pltpu.make_async_copy(
            x_ref.at[:, pl.ds(first, CHUNK)], tails.at[device], tail_sem
        ).start()
        return 0

    lax.fori_loop(0, n, load_tail, 0)

    barrier = pltpu.get_barrier_semaphore()

    def greet(i, _):
        pl.semaphore_signal(
            barrier, inc=1, device_id={"seq": lax.rem(me + i, n)}, device_id_type=MESH
        )
        return 0

    lax.fori_loop(1, n, greet, 0)
    pl.semaphore_wait(barrier, n - 1)

    def peer(i, shift):
        move = lax.rem(i * 11 + shift, n - 1) + 1
        if n != 32:
            return lax.rem(me + move, n)
        y = lax.rem(me // 8 + move // 8, 4)
        x = lax.rem(me // 2 + move // 2, 4)
        core = lax.rem(me + move, 2)
        return y * 8 + x * 2 + core

    def piece(device, c):
        first = pl.multiple_of(device * (CHUNK * CHUNKS) + c * CHUNK, CHUNK)
        return x_ref.at[pl.ds(0, body), pl.ds(first, CHUNK)]

    def send_chunk(c, _):

        def send(i, _):
            device = peer(i, c * 5)
            pltpu.make_async_remote_copy(
                src_ref=piece(device, c),
                dst_ref=recv.at[c, me],
                send_sem=chunk_send.at[c],
                recv_sem=chunk_recv.at[c],
                device_id={"seq": device},
                device_id_type=MESH,
            ).start()
            return 0

        lax.fori_loop(0, n - 1, send, 0)
        pltpu.make_async_copy(piece(me, c), recv.at[c, me], chunk_own.at[c]).start()
        return 0

    send_chunk(0, 0)
    pltpu.make_async_copy(tails, tails, tail_sem).wait()
    spare_load.wait()

    def make_extra(device, _):
        before = lax.rem(device + n - 1, n)
        has_past = jnp.where(device > 0, 1.0, 0.0).astype(F32)
        tail = tails[before].astype(F32) * has_past
        first = jnp.transpose(tail[:CHUNK, :])
        second = jnp.transpose(
            jnp.concatenate([tail[CHUNK:, :], jnp.zeros((2 * CHUNK - slab, CHUNK), F32)], axis=0)
        )
        held = [
            spare[
                :, pl.ds(pl.multiple_of(device * (CHUNK * CHUNKS) + c * CHUNK, CHUNK), CHUNK)
            ].astype(F32)
            for c in range(CHUNKS)
        ]
        extra_out[device] = jnp.concatenate(
            held + [first[CHUNK - 3 :, :], second[CHUNK - 3 :, :], jnp.zeros((2, CHUNK), F32)],
            axis=0,
        ).astype(BF16)
        return 0

    lax.fori_loop(0, n, make_extra, 0)

    def send_extra(i, _):
        device = peer(i, 0)
        pltpu.make_async_remote_copy(
            src_ref=extra_out.at[device],
            dst_ref=extra_in.at[me],
            send_sem=extra_send,
            recv_sem=extra_recv,
            device_id={"seq": device},
            device_id_type=MESH,
        ).start()
        return 0

    lax.fori_loop(0, n - 1, send_extra, 0)
    extra_in[me] = extra_out[me]
    lax.fori_loop(1, AHEAD + 1, send_chunk, 0)

    def wait_chunk(c):
        peers = recv.at[c, pl.ds(0, n - 1)]
        pltpu.make_async_copy(peers, peers, chunk_recv.at[c]).wait()
        pltpu.make_async_copy(recv.at[c, 0], recv.at[c, 0], chunk_own.at[c]).wait()

    sub = lax.broadcasted_iota(jnp.int32, (CHUNK, CHUNK), 0)
    lane = lax.broadcasted_iota(jnp.int32, (CHUNK, CHUNK), 1)
    causal = sub <= lane

    load.wait()

    def taps_of(g, i):
        four = jnp.concatenate(
            [
                pack_ref[pl.ds((k * GROUPS + g) * (CONV // CHUNK) + i, 1), :]
                for k in range(4)
            ]
            + [jnp.zeros((CHUNK - 4, CHUNK), F32)],
            axis=0,
        )
        turned = jnp.transpose(four)
        for k in range(4):
            taps[g, k, i * CHUNK : (i + 1) * CHUNK, :] = jnp.broadcast_to(
                turned[:, k : k + 1], (CHUNK, CHUNK)
            )

    for g in range(GROUPS):
        for i in range(CONV // CHUNK):
            taps_of(g, i)
    rows[0:CHUNK, :] = jnp.zeros((CHUNK, CHUNK), F32)
    rows[0:8, :] = pack_ref[CONV_ROWS : CONV_ROWS + 8, :]
    turned = jnp.transpose(rows[0:CHUNK, :])
    for k in range(3):
        for g in range(GROUPS):
            params[k, g] = jnp.broadcast_to(
                turned[g * HEADS : (g + 1) * HEADS, k : k + 1], (HEADS, CHUNK)
            )
    lead[...] = jnp.zeros_like(lead)
    state[...] = jnp.zeros_like(state)

    def lay_rows(target, c, g, first, end):
        for k in range(first, end):
            target[k * slab : k * slab + body, :] = recv[c, g * per_group + k].astype(F32)
            target[k * slab + body : (k + 1) * slab, :] = extra[
                g * per_group + k, pl.ds(c, 1), :
            ]

    def lay_out(c, g):
        lay_rows(rows, c, g, SPAN // slab, per_group)

    def lay_out_gates(c, g):
        lay_rows(gates, c, g, 0, -(-SPAN // slab))

    extras = extra_in.at[pl.ds(0, n - 1)]
    pltpu.make_async_copy(extras, extras, extra_recv).wait()

    def read_extra(device, _):
        extra[device] = extra_in[device].astype(F32)[:CHUNKS, :]
        return 0

    lax.fori_loop(0, n, read_extra, 0)
    blank = jnp.zeros((CHUNK - 3, CHUNK), F32)

    def read_past(g, _):
        for k in range(SPAN // slab, per_group):
            message = extra_in[g * per_group + k].astype(F32)
            first = jnp.transpose(jnp.concatenate([blank, message[8:11, :]], axis=0))
            second = jnp.transpose(jnp.concatenate([blank, message[11:14, :]], axis=0))
            rows[k * slab : k * slab + CHUNK, :] = first
            rows[k * slab + CHUNK : (k + 1) * slab, :] = second[: slab - CHUNK, :]
        for i in range(CONV // CHUNK):
            span = slice(i * CHUNK, (i + 1) * CHUNK)
            prev[g, span, :] = rows[SPAN + i * CHUNK : SPAN + (i + 1) * CHUNK, :]
        return 0

    lax.fori_loop(0, GROUPS, read_past, 0)

    def advance(u, _):
        c = u // GROUPS
        g = lax.rem(u, GROUPS)
        slot = lax.rem(u, HELD)

        @pl.when(g == 0)
        def _():
            wait_chunk(c)

            @pl.when(c + 1 + AHEAD < CHUNKS)
            def _():
                send_chunk(c + 1 + AHEAD, 0)

        lay_out(c, g)
        for i in range(CONV // CHUNK):
            span = slice(i * CHUNK, (i + 1) * CHUNK)
            current = rows[SPAN + i * CHUNK : SPAN + (i + 1) * CHUNK, :]
            past = prev[g, span, :]
            total = taps[g, 3, span, :] * current
            for k in range(1, 4):
                shifted = pltpu.roll(jnp.where(lane >= CHUNK - k, past, current), k, 1)
                total += taps[g, 3 - k, span, :] * shifted
            prev[g, span, :] = current
            value = silu(total)
            if i < SPAN // CHUNK:
                act[slot, span, :] = value.astype(BF16)
            elif i == SPAN // CHUNK:
                into[slot] = jnp.transpose(value).astype(BF16)
            else:
                outmap[slot] = value.astype(BF16)
                outrows[u] = jnp.transpose(value).astype(BF16)

        raw = rows[SPAN + CONV : COLS, :] + params[0, g]
        step = jnp.maximum(raw, 0.0) + jnp.log1p(jnp.exp(-jnp.abs(raw)))
        log_decay = -jnp.exp(params[1, g]) * step
        running = dot(log_decay, causal.astype(F32), lax.Precision.HIGHEST)
        last = jnp.broadcast_to(running[:, CHUNK - 1 :], (HEADS, CHUNK))
        until = jnp.exp(last - running) * step
        fade = jnp.exp(last)
        small[slot, 0] = running
        small[slot, 1] = jnp.exp(running)
        small[slot, 2] = jnp.exp(running + lead[g])
        lead[g] += last
        within[slot] = jnp.transpose(
            jnp.concatenate(
                [running - jnp.log(step), jnp.zeros((CHUNK - HEADS, CHUNK), F32)], axis=0
            )
        )
        cmat = outmap[slot]
        high = state[g].astype(BF16)
        low = (state[g] - high.astype(F32)).astype(BF16)
        carried[slot] = dot(
            jnp.concatenate([high, low], axis=1), jnp.concatenate([cmat, cmat], axis=0)
        )
        for h in range(HEADS):
            span = slice(h * HEAD_DIM, (h + 1) * HEAD_DIM)
            wgt[span, :] = (act[slot, span, :].astype(F32) * until[h : h + 1, :]).astype(BF16)
        update = dot(wgt[...], into[slot])
        for h in range(HEADS):
            span = slice(h * HEAD_DIM, (h + 1) * HEAD_DIM)
            state[g, span, :] = state[g, span, :] * fade[h : h + 1, :] + update[span, :]
        return 0

    def mix(u, _):
        c = u // GROUPS
        g = lax.rem(u, GROUPS)
        slot = lax.rem(u, HELD)
        lay_out_gates(c, g)
        scores = dot(into[slot], outmap[slot])
        columns = within[slot]
        for pair in range(HEADS // 2):
            owns = []
            reaches = []
            for h in (2 * pair, 2 * pair + 1):
                span = slice(h * HEAD_DIM, (h + 1) * HEAD_DIM)
                gaps = small[slot, 0, h : h + 1, :] - columns[:, h : h + 1]
                weights = (scores * jnp.exp(jnp.where(causal, gaps, -jnp.inf))).astype(BF16)
                x = act[slot, span, :]
                mixed = (
                    dot(x, weights)
                    + params[2, g, h : h + 1, :] * x.astype(F32)
                    + carried[slot, span, :] * small[slot, 1, h : h + 1, :]
                )
                gate = silu(gates[span, :])
                owns.append(mixed * gate)
                reaches.append(gate * small[slot, 2, h : h + 1, :])
            span = slice(pair * 2 * HEAD_DIM, (pair + 1) * 2 * HEAD_DIM)
            turned_own[u, :, span] = jnp.transpose(jnp.concatenate(owns, axis=0))
            turned_gate[u, :, span] = jnp.transpose(jnp.concatenate(reaches, axis=0))
        return 0

    def unit(u, _):
        advance(u, 0)
        mix(u, 0)
        return 0

    units = CHUNKS * GROUPS
    lax.fori_loop(0, units - HELD, unit, 0)
    lax.fori_loop(units - HELD, units, advance, 0)

    low_sub = lax.broadcasted_iota(jnp.int32, (16, CHUNK), 0)
    for g in range(GROUPS):
        for h in range(HEADS):
            first = (g * HEADS + h) * MESSAGE
            own[first : first + HEAD_DIM, :] = state[
                g, h * HEAD_DIM : (h + 1) * HEAD_DIM, :
            ].astype(BF16)
            fade = jnp.broadcast_to(jnp.exp(lead[g, h : h + 1, :]), (16, CHUNK))
            high = fade.astype(BF16).astype(F32)
            middle = (fade - high).astype(BF16).astype(F32)
            parts = jnp.where(
                low_sub == 0,
                high,
                jnp.where(
                    low_sub == 1, middle, jnp.where(low_sub == 2, fade - high - middle, 0.0)
                ),
            )
            own[first + HEAD_DIM : first + MESSAGE, :] = parts.astype(BF16)

    def heads_of(ref, device, height):
        size = per_device * height
        return ref.at[pl.ds(pl.multiple_of(device * size, size), size)]

    def wait_all(ref, sem, height):
        peers = ref.at[pl.ds(0, (n - 1) * per_device * height)]
        pltpu.make_async_copy(peers, peers, sem).wait()

    def send_heads(source, target, height, send_sem, recv_sem):
        def send(i, _):
            device = peer(i, 0)
            pltpu.make_async_remote_copy(
                src_ref=heads_of(source, device, height),
                dst_ref=heads_of(target, me, height),
                send_sem=send_sem,
                recv_sem=recv_sem,
                device_id={"seq": device},
                device_id_type=MESH,
            ).start()
            return 0

        lax.fori_loop(0, n - 1, send, 0)
        heads_of(target, me, height)[...] = heads_of(source, me, height)[...]

    send_heads(own, gathered, MESSAGE, scan_send, scan_recv)
    lax.fori_loop(units - HELD, units, mix, 0)
    wait_all(gathered, scan_recv, MESSAGE)

    def horner(device, reached):
        heads_of(prefix, device, HEAD_DIM)[...] = reached.astype(BF16)
        message = heads_of(gathered, device, MESSAGE)[...].astype(F32)
        terms = []
        for h in range(per_device):
            first = h * MESSAGE
            fade = jnp.sum(message[first + HEAD_DIM : first + MESSAGE, :], axis=0, keepdims=True)
            terms.append(
                reached[h * HEAD_DIM : (h + 1) * HEAD_DIM, :] * fade
                + message[first : first + HEAD_DIM, :]
            )
        return terms[0] if per_device == 1 else jnp.concatenate(terms, axis=0)

    lax.fori_loop(0, n, horner, jnp.zeros((per_device * HEAD_DIM, STATE_WIDTH), F32))
    send_heads(prefix, incoming, HEAD_DIM, back_send, back_recv)
    wait_all(incoming, back_recv, HEAD_DIM)

    def finish(u, _):
        c = u // GROUPS
        g = lax.rem(u, GROUPS)
        gain = jnp.concatenate(
            [
                pack_ref[pl.ds(CONV_ROWS + 8 + g * (SPAN // CHUNK) + i, 1), :]
                for i in range(SPAN // CHUNK)
            ],
            axis=1,
        )
        arrived = dot_nt(
            outrows[u], incoming[pl.ds(pl.multiple_of(g * SPAN, SPAN), SPAN), :]
        )
        for i in range(CHUNK // 16):
            span = slice(i * 16, (i + 1) * 16)
            gated = turned_own[u, span, :] + arrived[span, :] * turned_gate[u, span, :]
            squares = jnp.sum(gated * gated, axis=1, keepdims=True)
            scale = lax.rsqrt(squares * (1.0 / SPAN) + EPSILON)
            staged[u, span, :] = (gated * scale * gain).astype(BF16)
        pltpu.make_async_copy(
            staged.at[u],
            out_ref.at[
                pl.ds(pl.multiple_of(c * CHUNK, CHUNK), CHUNK),
                pl.ds(pl.multiple_of(g * SPAN, SPAN), SPAN),
            ],
            out_sem,
        ).start()
        return 0

    lax.fori_loop(0, units, finish, 0)

    def drain(c, _):
        peers = recv.at[c, pl.ds(0, n - 1)]
        pltpu.make_async_copy(peers, peers, chunk_send.at[c]).wait()
        return 0

    lax.fori_loop(0, CHUNKS, drain, 0)
    pltpu.make_async_copy(extras, extras, extra_send).wait()
    wait_all(own, scan_send, MESSAGE)
    wait_all(prefix, back_send, HEAD_DIM)
    pltpu.make_async_copy(staged, staged, out_sem).wait()


def per_device(projected, conv_weight, dt_bias, a_log, d_skip, norm_gain):
    n = lax.axis_size("seq")
    slab = COLS * GROUPS // n
    tokens = CHUNK * CHUNKS
    units = GROUPS * CHUNKS
    heads = GROUPS * HEADS
    scalars = jnp.stack([dt_bias, a_log, d_skip])
    packed = jnp.concatenate(
        [
            conv_weight.reshape(-1, CHUNK),
            jnp.pad(scalars, ((0, 5), (0, CHUNK - heads))),
            norm_gain.reshape(-1, CHUNK),
        ],
        axis=0,
    )
    hbm = pl.BlockSpec(memory_space=pltpu.HBM)
    anywhere = pl.BlockSpec(memory_space=pl.ANY)
    dma = pltpu.SemaphoreType.DMA
    return pl.pallas_call(
        functools.partial(kernel, n),
        out_shape=jax.ShapeDtypeStruct((tokens, GROUPS * SPAN), BF16),
        in_specs=[hbm] * 2,
        out_specs=anywhere,
        scratch_shapes=[
            pltpu.VMEM(packed.shape, F32),
            pltpu.VMEM((CHUNKS, n, slab - 1, CHUNK), BF16),
            pltpu.VMEM((COLS, CHUNK), F32),
            pltpu.VMEM((-(-SPAN // slab) * slab, CHUNK), F32),
            pltpu.VMEM((GROUPS, 4, CONV, CHUNK), F32),
            pltpu.VMEM((3, GROUPS, HEADS, CHUNK), F32),
            pltpu.VMEM((GROUPS, CONV, CHUNK), F32),
            pltpu.VMEM((HELD, SPAN, CHUNK), BF16),
            pltpu.VMEM((SPAN, CHUNK), BF16),
            pltpu.VMEM((GROUPS, SPAN, STATE_WIDTH), F32),
            pltpu.VMEM((HELD, SPAN, CHUNK), F32),
            pltpu.VMEM((HELD, CHUNK, CHUNK), F32),
            pltpu.VMEM((HELD, CHUNK, STATE_WIDTH), BF16),
            pltpu.VMEM((HELD, STATE_WIDTH, CHUNK), BF16),
            pltpu.VMEM((units, CHUNK, STATE_WIDTH), BF16),
            pltpu.VMEM((HELD, 3, HEADS, CHUNK), F32),
            pltpu.VMEM((GROUPS, HEADS, CHUNK), F32),
            pltpu.VMEM((units, CHUNK, SPAN), F32),
            pltpu.VMEM((units, CHUNK, SPAN), F32),
            pltpu.VMEM((n, slab, CHUNK), BF16),
            pltpu.VMEM((1, n * tokens), BF16),
            pltpu.VMEM((n, 16, CHUNK), BF16),
            pltpu.VMEM((n, 16, CHUNK), BF16),
            pltpu.VMEM((n, CHUNKS, CHUNK), F32),
            pltpu.VMEM((heads * MESSAGE, STATE_WIDTH), BF16),
            pltpu.VMEM((heads * MESSAGE, STATE_WIDTH), BF16),
            pltpu.VMEM((heads * HEAD_DIM, STATE_WIDTH), BF16),
            pltpu.VMEM((heads * HEAD_DIM, STATE_WIDTH), BF16),
            pltpu.VMEM((units, CHUNK, SPAN), BF16),
            dma((CHUNKS,)), dma((CHUNKS,)), dma((CHUNKS,)), dma, dma, dma, dma,
            dma, dma, dma, dma, dma, dma,
        ],
        compiler_params=pltpu.CompilerParams(
            collective_id=0, has_side_effects=True, vmem_limit_bytes=48 * 2**20
        ),
    )(
        projected, packed
    )


def solution(mesh):
    in_specs = (P(("tp", "seq"), None), P(None, "tp", None), P("tp"), P("tp"), P("tp"), P("tp"))
    return jax.shard_map(
        per_device, mesh=mesh, in_specs=in_specs, out_specs=P("seq", "tp"), check_vma=False
    )
```

```python
import functools

import jax
import jax.numpy as jnp
from jax import lax
from jax.experimental import pallas as pl
from jax.experimental.pallas import tpu as pltpu
from jax.sharding import PartitionSpec as P

MESH = pl.DeviceIdType.MESH
HEAD_DIM = 64
STATE_WIDTH = 128
CHUNK = 128
CHUNKS = 8
GROUPS = 2
HEADS = 16
SPAN = HEADS * HEAD_DIM
CONV = SPAN + 2 * STATE_WIDTH
COLS = SPAN + CONV + HEADS
EPSILON = 1e-05
AHEAD = 3
CONV_ROWS = 4 * GROUPS * CONV // CHUNK
HELD = 2
MESSAGE = HEAD_DIM + 16

F32 = jnp.float32
BF16 = jnp.bfloat16


def silu(v):
    return v * (1.0 / (1.0 + jnp.exp(-v)))


def dot(a, b, precision=None):
    return jnp.dot(a, b, preferred_element_type=F32, precision=precision)


def kernel(
    n, x_ref, pack_hbm, out_ref,
    pack_ref, recv, rows, gates, taps, params, prev, act, wgt, state, carried, within, into,
    outmap, outrows, small, lead, turned_gate, turned_own,
    tails, spare, extra_out, extra_in, extra, own, gathered, prefix, incoming, turned_in, staged,
    chunk_send, chunk_recv, chunk_own, extra_send, extra_recv, tail_sem, spare_sem,
    scan_send, scan_recv, back_send, back_recv, out_sem, small_sem,
):
    me = lax.axis_index("seq")
    slab = COLS * GROUPS // n
    body = slab - 1
    per_group = n // GROUPS

    load = pltpu.make_async_copy(pack_hbm, pack_ref, small_sem)
    load.start()
    spare_load = pltpu.make_async_copy(x_ref.at[pl.ds(body, 1), :], spare, spare_sem)
    spare_load.start()

    def load_tail(device, _):
        first = pl.multiple_of((device + 1) * CHUNK * CHUNKS - CHUNK, CHUNK)
        pltpu.make_async_copy(
            x_ref.at[:, pl.ds(first, CHUNK)], tails.at[device], tail_sem
        ).start()
        return 0

    lax.fori_loop(0, n, load_tail, 0)

    barrier = pltpu.get_barrier_semaphore()

    def greet(i, _):
        pl.semaphore_signal(
            barrier, inc=1, device_id={"seq": lax.rem(me + i, n)}, device_id_type=MESH
        )
        return 0

    lax.fori_loop(1, n, greet, 0)
    pl.semaphore_wait(barrier, n - 1)

    def peer(i, shift):
        move = lax.rem(i * 11 + shift, n - 1) + 1
        if n != 32:
            return lax.rem(me + move, n)
        y = lax.rem(me // 8 + move // 8, 4)
        x = lax.rem(me // 2 + move // 2, 4)
        core = lax.rem(me + move, 2)
        return y * 8 + x * 2 + core

    def piece(device, c):
        first = pl.multiple_of(device * (CHUNK * CHUNKS) + c * CHUNK, CHUNK)
        return x_ref.at[pl.ds(0, body), pl.ds(first, CHUNK)]

    def send_chunk(c, _):

        def send(i, _):
            device = peer(i, c * 5)
            pltpu.make_async_remote_copy(
                src_ref=piece(device, c),
                dst_ref=recv.at[c, me],
                send_sem=chunk_send.at[c],
                recv_sem=chunk_recv.at[c],
                device_id={"seq": device},
                device_id_type=MESH,
            ).start()
            return 0

        lax.fori_loop(0, n - 1, send, 0)
        pltpu.make_async_copy(piece(me, c), recv.at[c, me], chunk_own.at[c]).start()
        return 0

    send_chunk(0, 0)
    pltpu.make_async_copy(tails, tails, tail_sem).wait()
    spare_load.wait()

    def make_extra(device, _):
        before = lax.rem(device + n - 1, n)
        has_past = jnp.where(device > 0, 1.0, 0.0).astype(F32)
        tail = tails[before].astype(F32) * has_past
        first = jnp.transpose(tail[:CHUNK, :])
        second = jnp.transpose(
            jnp.concatenate([tail[CHUNK:, :], jnp.zeros((2 * CHUNK - slab, CHUNK), F32)], axis=0)
        )
        held = [
            spare[
                :, pl.ds(pl.multiple_of(device * (CHUNK * CHUNKS) + c * CHUNK, CHUNK), CHUNK)
            ].astype(F32)
            for c in range(CHUNKS)
        ]
        extra_out[device] = jnp.concatenate(
            held + [first[CHUNK - 3 :, :], second[CHUNK - 3 :, :], jnp.zeros((2, CHUNK), F32)],
            axis=0,
        ).astype(BF16)
        return 0

    lax.fori_loop(0, n, make_extra, 0)

    def send_extra(i, _):
        device = peer(i, 0)
        pltpu.make_async_remote_copy(
            src_ref=extra_out.at[device],
            dst_ref=extra_in.at[me],
            send_sem=extra_send,
            recv_sem=extra_recv,
            device_id={"seq": device},
            device_id_type=MESH,
        ).start()
        return 0

    lax.fori_loop(0, n - 1, send_extra, 0)
    extra_in[me] = extra_out[me]
    lax.fori_loop(1, AHEAD + 1, send_chunk, 0)

    def wait_chunk(c):
        peers = recv.at[c, pl.ds(0, n - 1)]
        pltpu.make_async_copy(peers, peers, chunk_recv.at[c]).wait()
        pltpu.make_async_copy(recv.at[c, 0], recv.at[c, 0], chunk_own.at[c]).wait()

    sub = lax.broadcasted_iota(jnp.int32, (CHUNK, CHUNK), 0)
    lane = lax.broadcasted_iota(jnp.int32, (CHUNK, CHUNK), 1)
    causal = sub <= lane

    load.wait()

    def taps_of(g, i):
        four = jnp.concatenate(
            [
                pack_ref[pl.ds((k * GROUPS + g) * (CONV // CHUNK) + i, 1), :]
                for k in range(4)
            ]
            + [jnp.zeros((CHUNK - 4, CHUNK), F32)],
            axis=0,
        )
        turned = jnp.transpose(four)
        for k in range(4):
            taps[g, k, i * CHUNK : (i + 1) * CHUNK, :] = jnp.broadcast_to(
                turned[:, k : k + 1], (CHUNK, CHUNK)
            )

    for g in range(GROUPS):
        for i in range(CONV // CHUNK):
            taps_of(g, i)
    rows[0:CHUNK, :] = jnp.zeros((CHUNK, CHUNK), F32)
    rows[0:8, :] = pack_ref[CONV_ROWS : CONV_ROWS + 8, :]
    turned = jnp.transpose(rows[0:CHUNK, :])
    for k in range(3):
        for g in range(GROUPS):
            params[k, g] = jnp.broadcast_to(
                turned[g * HEADS : (g + 1) * HEADS, k : k + 1], (HEADS, CHUNK)
            )
    lead[...] = jnp.zeros_like(lead)
    state[...] = jnp.zeros_like(state)

    def lay_rows(target, c, g, first, end):
        for k in range(first, end):
            target[k * slab : k * slab + body, :] = recv[c, g * per_group + k].astype(F32)
            target[k * slab + body : (k + 1) * slab, :] = extra[
                g * per_group + k, pl.ds(c, 1), :
            ]

    def lay_out(c, g):
        lay_rows(rows, c, g, SPAN // slab, per_group)

    def lay_out_gates(c, g):
        lay_rows(gates, c, g, 0, -(-SPAN // slab))

    extras = extra_in.at[pl.ds(0, n - 1)]
    pltpu.make_async_copy(extras, extras, extra_recv).wait()

    def read_extra(device, _):
        extra[device] = extra_in[device].astype(F32)[:CHUNKS, :]
        return 0

    lax.fori_loop(0, n, read_extra, 0)
    blank = jnp.zeros((CHUNK - 3, CHUNK), F32)

    def read_past(g, _):
        for k in range(SPAN // slab, per_group):
            message = extra_in[g * per_group + k].astype(F32)
            first = jnp.transpose(jnp.concatenate([blank, message[8:11, :]], axis=0))
            second = jnp.transpose(jnp.concatenate([blank, message[11:14, :]], axis=0))
            rows[k * slab : k * slab + CHUNK, :] = first
            rows[k * slab + CHUNK : (k + 1) * slab, :] = second[: slab - CHUNK, :]
        for i in range(CONV // CHUNK):
            span = slice(i * CHUNK, (i + 1) * CHUNK)
            prev[g, span, :] = rows[SPAN + i * CHUNK : SPAN + (i + 1) * CHUNK, :]
        return 0

    lax.fori_loop(0, GROUPS, read_past, 0)

    def advance(u, _):
        c = u // GROUPS
        g = lax.rem(u, GROUPS)
        slot = lax.rem(u, HELD)

        @pl.when(g == 0)
        def _():
            wait_chunk(c)

            @pl.when(c + 1 + AHEAD < CHUNKS)
            def _():
                send_chunk(c + 1 + AHEAD, 0)

        lay_out(c, g)
        for i in range(CONV // CHUNK):
            span = slice(i * CHUNK, (i + 1) * CHUNK)
            current = rows[SPAN + i * CHUNK : SPAN + (i + 1) * CHUNK, :]
            past = prev[g, span, :]
            total = taps[g, 3, span, :] * current
            for k in range(1, 4):
                shifted = pltpu.roll(jnp.where(lane >= CHUNK - k, past, current), k, 1)
                total += taps[g, 3 - k, span, :] * shifted
            prev[g, span, :] = current
            value = silu(total)
            if i < SPAN // CHUNK:
                act[slot, span, :] = value.astype(BF16)
            elif i == SPAN // CHUNK:
                into[slot] = jnp.transpose(value).astype(BF16)
            else:
                outmap[slot] = value.astype(BF16)
                outrows[u] = jnp.transpose(value).astype(BF16)

        raw = rows[SPAN + CONV : COLS, :] + params[0, g]
        step = jnp.maximum(raw, 0.0) + jnp.log1p(jnp.exp(-jnp.abs(raw)))
        log_decay = -jnp.exp(params[1, g]) * step
        running = dot(log_decay, causal.astype(F32), lax.Precision.HIGHEST)
        last = jnp.broadcast_to(running[:, CHUNK - 1 :], (HEADS, CHUNK))
        until = jnp.exp(last - running) * step
        fade = jnp.exp(last)
        small[slot, 0] = running
        small[slot, 1] = jnp.exp(running)
        small[slot, 2] = jnp.exp(running + lead[g])
        lead[g] += last
        within[slot] = jnp.transpose(
            jnp.concatenate(
                [running - jnp.log(step), jnp.zeros((CHUNK - HEADS, CHUNK), F32)], axis=0
            )
        )
        cmat = outmap[slot]
        high = state[g].astype(BF16)
        low = (state[g] - high.astype(F32)).astype(BF16)
        carried[slot] = dot(
            jnp.concatenate([high, low], axis=1), jnp.concatenate([cmat, cmat], axis=0)
        )
        for h in range(HEADS):
            span = slice(h * HEAD_DIM, (h + 1) * HEAD_DIM)
            wgt[span, :] = (act[slot, span, :].astype(F32) * until[h : h + 1, :]).astype(BF16)
        update = dot(wgt[...], into[slot])
        for h in range(HEADS):
            span = slice(h * HEAD_DIM, (h + 1) * HEAD_DIM)
            state[g, span, :] = state[g, span, :] * fade[h : h + 1, :] + update[span, :]
        return 0

    def mix(u, _):
        c = u // GROUPS
        g = lax.rem(u, GROUPS)
        slot = lax.rem(u, HELD)
        lay_out_gates(c, g)
        scores = dot(into[slot], outmap[slot])
        columns = within[slot]
        for pair in range(HEADS // 2):
            owns = []
            reaches = []
            for h in (2 * pair, 2 * pair + 1):
                span = slice(h * HEAD_DIM, (h + 1) * HEAD_DIM)
                gaps = small[slot, 0, h : h + 1, :] - columns[:, h : h + 1]
                weights = (scores * jnp.exp(jnp.where(causal, gaps, -jnp.inf))).astype(BF16)
                x = act[slot, span, :]
                mixed = (
                    dot(x, weights)
                    + params[2, g, h : h + 1, :] * x.astype(F32)
                    + carried[slot, span, :] * small[slot, 1, h : h + 1, :]
                )
                gate = silu(gates[span, :])
                owns.append(mixed * gate)
                reaches.append(gate * small[slot, 2, h : h + 1, :])
            span = slice(pair * 2 * HEAD_DIM, (pair + 1) * 2 * HEAD_DIM)
            turned_own[u, :, span] = jnp.transpose(jnp.concatenate(owns, axis=0))
            turned_gate[u, :, span] = jnp.transpose(jnp.concatenate(reaches, axis=0))
        return 0

    def unit(u, _):
        advance(u, 0)
        mix(u, 0)
        return 0

    units = CHUNKS * GROUPS
    lax.fori_loop(0, units - HELD, unit, 0)

    low_sub = lax.broadcasted_iota(jnp.int32, (16, CHUNK), 0)

    def head_at(ref, position, height):
        return ref.at[pl.ds(pl.multiple_of(position * height, height), height)]

    def wait_messages(ref, count, height, sem):
        messages = ref.at[pl.ds(0, count * height)]
        pltpu.make_async_copy(messages, messages, sem).wait()

    mine = lax.rem(me, GROUPS)
    for g in range(GROUPS):
        advance(units - HELD + g, 0)
        for h in range(HEADS):
            first = (h * GROUPS + g) * MESSAGE
            own[first : first + HEAD_DIM, :] = state[
                g, h * HEAD_DIM : (h + 1) * HEAD_DIM, :
            ].astype(BF16)
            fade = jnp.broadcast_to(jnp.exp(lead[g, h : h + 1, :]), (16, CHUNK))
            high = fade.astype(BF16).astype(F32)
            middle = (fade - high).astype(BF16).astype(F32)
            parts = jnp.where(
                low_sub == 0,
                high,
                jnp.where(
                    low_sub == 1, middle, jnp.where(low_sub == 2, fade - high - middle, 0.0)
                ),
            )
            own[first + HEAD_DIM : first + MESSAGE, :] = parts.astype(BF16)

        def send_state(i, _):
            move = lax.rem(i * 5 + 6, HEADS)
            y = lax.rem(me // 8 + move // 4, 4)
            x = lax.rem(me // 2 + move, 4)
            device = y * 8 + x * 2 + g

            @pl.when(device != me)
            def _():
                pltpu.make_async_remote_copy(
                    src_ref=head_at(own, device, MESSAGE),
                    dst_ref=head_at(gathered, me, MESSAGE),
                    send_sem=scan_send,
                    recv_sem=scan_recv,
                    device_id={"seq": device},
                    device_id_type=MESH,
                ).start()

            return 0

        lax.fori_loop(0, HEADS, send_state, 0)
    head_at(gathered, me, MESSAGE)[...] = head_at(own, me, MESSAGE)[...]

    @pl.when(mine == 1)
    def _():
        lax.fori_loop(units - HELD, units, mix, 0)

    wait_messages(gathered, n - 1, MESSAGE, scan_recv)

    def horner(device, reached):
        head_at(prefix, device, HEAD_DIM)[...] = reached.astype(BF16)
        message = head_at(gathered, device, MESSAGE)[...].astype(F32)
        fade = jnp.sum(message[HEAD_DIM:, :], axis=0, keepdims=True)
        return reached * fade + message[:HEAD_DIM, :]

    lax.fori_loop(0, n, horner, jnp.zeros((HEAD_DIM, STATE_WIDTH), F32))
    slot = mine * HEADS + me // GROUPS

    def send_back(i, _):
        device = peer(i, 0)
        pltpu.make_async_remote_copy(
            src_ref=head_at(prefix, device, HEAD_DIM),
            dst_ref=head_at(incoming, slot, HEAD_DIM),
            send_sem=back_send,
            recv_sem=back_recv.at[mine],
            device_id={"seq": device},
            device_id_type=MESH,
        ).start()
        return 0

    lax.fori_loop(0, n - 1, send_back, 0)
    head_at(incoming, slot, HEAD_DIM)[...] = head_at(prefix, me, HEAD_DIM)[...]

    @pl.when(mine == 0)
    def _():
        lax.fori_loop(units - HELD, units, mix, 0)

    for g in range(GROUPS):

        @pl.when(mine == g)
        def _():
            wait_messages(incoming, HEADS - 1, HEAD_DIM, back_recv.at[g])

        @pl.when(mine != g)
        def _():
            wait_messages(incoming, HEADS, HEAD_DIM, back_recv.at[g])

        for i in range(SPAN // CHUNK):
            block = incoming[g * SPAN + i * CHUNK : g * SPAN + (i + 1) * CHUNK, :]
            turned_in[:, i * CHUNK : (i + 1) * CHUNK] = jnp.transpose(block.astype(F32)).astype(
                BF16
            )
        first = CONV_ROWS + 8 + g * (SPAN // CHUNK)
        gain = jnp.concatenate(
            [pack_ref[first + i : first + i + 1, :] for i in range(SPAN // CHUNK)], axis=1
        )

        def finish(c, _):
            u = c * GROUPS + g
            arrived = dot(outrows[u], turned_in[...])
            for i in range(CHUNK // 16):
                span = slice(i * 16, (i + 1) * 16)
                gated = turned_own[u, span, :] + arrived[span, :] * turned_gate[u, span, :]
                squares = jnp.sum(gated * gated, axis=1, keepdims=True)
                scale = lax.rsqrt(squares * (1.0 / SPAN) + EPSILON)
                staged[u, span, :] = (gated * scale * gain).astype(BF16)
            pltpu.make_async_copy(
                staged.at[u],
                out_ref.at[
                    pl.ds(pl.multiple_of(c * CHUNK, CHUNK), CHUNK),
                    pl.ds(g * SPAN, SPAN),
                ],
                out_sem,
            ).start()
            return 0

        lax.fori_loop(0, CHUNKS, finish, 0)

    def drain(c, _):
        peers = recv.at[c, pl.ds(0, n - 1)]
        pltpu.make_async_copy(peers, peers, chunk_send.at[c]).wait()
        return 0

    lax.fori_loop(0, CHUNKS, drain, 0)
    pltpu.make_async_copy(extras, extras, extra_send).wait()
    wait_messages(own, n - 1, MESSAGE, scan_send)
    wait_messages(prefix, n - 1, HEAD_DIM, back_send)
    pltpu.make_async_copy(staged, staged, out_sem).wait()


def per_device(projected, conv_weight, dt_bias, a_log, d_skip, norm_gain):
    n = lax.axis_size("seq")
    slab = COLS * GROUPS // n
    tokens = CHUNK * CHUNKS
    units = GROUPS * CHUNKS
    heads = GROUPS * HEADS
    scalars = jnp.stack([dt_bias, a_log, d_skip])
    packed = jnp.concatenate(
        [
            conv_weight.reshape(-1, CHUNK),
            jnp.pad(scalars, ((0, 5), (0, CHUNK - heads))),
            norm_gain.reshape(-1, CHUNK),
        ],
        axis=0,
    )
    hbm = pl.BlockSpec(memory_space=pltpu.HBM)
    anywhere = pl.BlockSpec(memory_space=pl.ANY)
    dma = pltpu.SemaphoreType.DMA
    return pl.pallas_call(
        functools.partial(kernel, n),
        out_shape=jax.ShapeDtypeStruct((tokens, GROUPS * SPAN), BF16),
        in_specs=[hbm] * 2,
        out_specs=anywhere,
        scratch_shapes=[
            pltpu.VMEM(packed.shape, F32),
            pltpu.VMEM((CHUNKS, n, slab - 1, CHUNK), BF16),
            pltpu.VMEM((COLS, CHUNK), F32),
            pltpu.VMEM((-(-SPAN // slab) * slab, CHUNK), F32),
            pltpu.VMEM((GROUPS, 4, CONV, CHUNK), F32),
            pltpu.VMEM((3, GROUPS, HEADS, CHUNK), F32),
            pltpu.VMEM((GROUPS, CONV, CHUNK), F32),
            pltpu.VMEM((HELD, SPAN, CHUNK), BF16),
            pltpu.VMEM((SPAN, CHUNK), BF16),
            pltpu.VMEM((GROUPS, SPAN, STATE_WIDTH), F32),
            pltpu.VMEM((HELD, SPAN, CHUNK), F32),
            pltpu.VMEM((HELD, CHUNK, CHUNK), F32),
            pltpu.VMEM((HELD, CHUNK, STATE_WIDTH), BF16),
            pltpu.VMEM((HELD, STATE_WIDTH, CHUNK), BF16),
            pltpu.VMEM((units, CHUNK, STATE_WIDTH), BF16),
            pltpu.VMEM((HELD, 3, HEADS, CHUNK), F32),
            pltpu.VMEM((GROUPS, HEADS, CHUNK), F32),
            pltpu.VMEM((units, CHUNK, SPAN), F32),
            pltpu.VMEM((units, CHUNK, SPAN), F32),
            pltpu.VMEM((n, slab, CHUNK), BF16),
            pltpu.VMEM((1, n * tokens), BF16),
            pltpu.VMEM((n, 16, CHUNK), BF16),
            pltpu.VMEM((n, 16, CHUNK), BF16),
            pltpu.VMEM((n, CHUNKS, CHUNK), F32),
            pltpu.VMEM((heads * MESSAGE, STATE_WIDTH), BF16),
            pltpu.VMEM((heads * MESSAGE, STATE_WIDTH), BF16),
            pltpu.VMEM((heads * HEAD_DIM, STATE_WIDTH), BF16),
            pltpu.VMEM((heads * HEAD_DIM, STATE_WIDTH), BF16),
            pltpu.VMEM((STATE_WIDTH, SPAN), BF16),
            pltpu.VMEM((units, CHUNK, SPAN), BF16),
            dma((CHUNKS,)), dma((CHUNKS,)), dma((CHUNKS,)), dma, dma, dma, dma,
            dma, dma, dma, dma((GROUPS,)), dma, dma,
        ],
        compiler_params=pltpu.CompilerParams(
            collective_id=0, has_side_effects=True, vmem_limit_bytes=48 * 2**20
        ),
    )(
        projected, packed
    )


def solution(mesh):
    in_specs = (P(("tp", "seq"), None), P(None, "tp", None), P("tp"), P("tp"), P("tp"), P("tp"))
    return jax.shard_map(
        per_device, mesh=mesh, in_specs=in_specs, out_specs=P("seq", "tp"), check_vma=False
    )
```

```python
import functools

import jax
import jax.numpy as jnp
from jax import lax
from jax.experimental import pallas as pl
from jax.experimental.pallas import tpu as pltpu
from jax.sharding import PartitionSpec as P

MESH = pl.DeviceIdType.MESH
HEAD_DIM = 64
STATE_WIDTH = 128
CHUNK = 128
CHUNKS = 8
GROUPS = 2
HEADS = 16
SPAN = HEADS * HEAD_DIM
CONV = SPAN + 2 * STATE_WIDTH
COLS = SPAN + CONV + HEADS
EPSILON = 1e-05
AHEAD = 3
HELD = 2
MESSAGE = HEAD_DIM + 16

F32 = jnp.float32
BF16 = jnp.bfloat16


def silu(v):
    return v * (1.0 / (1.0 + jnp.exp(-v)))


def dot(a, b, precision=None):
    return jnp.dot(a, b, preferred_element_type=F32, precision=precision)


def kernel(
    n, x_ref, conv_hbm, pack_hbm, out_ref,
    conv_ref, pack_ref, recv, rows, gates, taps, params, prev, act, wgt, state, carried, within, into,
    outmap, outrows, small, lead, turned_gate, turned_own,
    tails, spare, extra_out, extra_in, extra, own, gathered, prefix, incoming, turned_in, staged,
    chunk_send, chunk_recv, chunk_own, extra_send, extra_recv, tail_sem, spare_sem,
    scan_send, scan_recv, back_send, back_recv, out_sem, small_sem,
):
    me = lax.axis_index("seq")
    slab = COLS * GROUPS // n
    body = slab - 1
    per_group = n // GROUPS

    loads = (
        pltpu.make_async_copy(pack_hbm, pack_ref, small_sem.at[0]),
        pltpu.make_async_copy(conv_hbm, conv_ref, small_sem.at[1]),
    )
    for load in loads:
        load.start()
    spare_load = pltpu.make_async_copy(x_ref.at[pl.ds(body, 1), :], spare, spare_sem)
    spare_load.start()

    def load_tail(device, _):
        first = pl.multiple_of((device + 1) * CHUNK * CHUNKS - CHUNK, CHUNK)
        pltpu.make_async_copy(
            x_ref.at[:, pl.ds(first, CHUNK)], tails.at[device], tail_sem
        ).start()
        return 0

    lax.fori_loop(0, n, load_tail, 0)

    barrier = pltpu.get_barrier_semaphore()

    def greet(i, _):
        pl.semaphore_signal(
            barrier, inc=1, device_id={"seq": lax.rem(me + i, n)}, device_id_type=MESH
        )
        return 0

    lax.fori_loop(1, n, greet, 0)
    pl.semaphore_wait(barrier, n - 1)

    def peer(i, shift):
        move = lax.rem(i * 17 + shift, n - 1) + 1
        if n != 32:
            return lax.rem(me + move, n)
        y = lax.rem(me // 8 + move // 8, 4)
        x = lax.rem(me // 2 + move // 2, 4)
        core = lax.rem(me + move, 2)
        return y * 8 + x * 2 + core

    def piece(device, c):
        first = pl.multiple_of(device * (CHUNK * CHUNKS) + c * CHUNK, CHUNK)
        return x_ref.at[pl.ds(0, body), pl.ds(first, CHUNK)]

    def send_chunk(c, _):

        def send(i, _):
            device = peer(i, c * 2)
            pltpu.make_async_remote_copy(
                src_ref=piece(device, c),
                dst_ref=recv.at[c, me],
                send_sem=chunk_send.at[c],
                recv_sem=chunk_recv.at[c],
                device_id={"seq": device},
                device_id_type=MESH,
            ).start()
            return 0

        lax.fori_loop(0, n - 1, send, 0)
        pltpu.make_async_copy(piece(me, c), recv.at[c, me], chunk_own.at[c]).start()
        return 0

    send_chunk(0, 0)
    pltpu.make_async_copy(tails, tails, tail_sem).wait()
    spare_load.wait()

    def make_extra(device, _):
        before = lax.rem(device + n - 1, n)
        has_past = jnp.where(device > 0, 1.0, 0.0).astype(F32)
        tail = tails[before].astype(F32) * has_past
        first = jnp.transpose(tail[:CHUNK, :])
        second = jnp.transpose(
            jnp.concatenate([tail[CHUNK:, :], jnp.zeros((2 * CHUNK - slab, CHUNK), F32)], axis=0)
        )
        held = [
            spare[
                :, pl.ds(pl.multiple_of(device * (CHUNK * CHUNKS) + c * CHUNK, CHUNK), CHUNK)
            ].astype(F32)
            for c in range(CHUNKS)
        ]
        extra_out[device] = jnp.concatenate(
            held + [first[CHUNK - 3 :, :], second[CHUNK - 3 :, :], jnp.zeros((2, CHUNK), F32)],
            axis=0,
        ).astype(BF16)
        return 0

    lax.fori_loop(0, n, make_extra, 0)

    def send_extra(i, _):
        device = peer(i, 0)
        pltpu.make_async_remote_copy(
            src_ref=extra_out.at[device],
            dst_ref=extra_in.at[me],
            send_sem=extra_send,
            recv_sem=extra_recv,
            device_id={"seq": device},
            device_id_type=MESH,
        ).start()
        return 0

    lax.fori_loop(0, n - 1, send_extra, 0)
    extra_in[me] = extra_out[me]
    lax.fori_loop(1, AHEAD + 1, send_chunk, 0)

    def wait_chunk(c):
        peers = recv.at[c, pl.ds(0, n - 1)]
        pltpu.make_async_copy(peers, peers, chunk_recv.at[c]).wait()
        pltpu.make_async_copy(recv.at[c, 0], recv.at[c, 0], chunk_own.at[c]).wait()

    sub = lax.broadcasted_iota(jnp.int32, (CHUNK, CHUNK), 0)
    lane = lax.broadcasted_iota(jnp.int32, (CHUNK, CHUNK), 1)
    causal = sub <= lane

    for load in loads:
        load.wait()

    def taps_of(g, i):
        four = jnp.concatenate(
            [
                conv_ref[k, g : g + 1, i * CHUNK : (i + 1) * CHUNK]
                for k in range(4)
            ]
            + [jnp.zeros((CHUNK - 4, CHUNK), F32)],
            axis=0,
        )
        turned = jnp.transpose(four)
        for k in range(4):
            taps[g, k, i * CHUNK : (i + 1) * CHUNK, :] = jnp.broadcast_to(
                turned[:, k : k + 1], (CHUNK, CHUNK)
            )

    for g in range(GROUPS):
        for i in range(CONV // CHUNK):
            taps_of(g, i)
    rows[0:CHUNK, :] = jnp.zeros((CHUNK, CHUNK), F32)
    for k in range(3):
        rows[k : k + 1, 0 : GROUPS * HEADS] = pack_ref[
            0:1, k * GROUPS * HEADS : (k + 1) * GROUPS * HEADS
        ]
    turned = jnp.transpose(rows[0:CHUNK, :])
    for k in range(3):
        for g in range(GROUPS):
            params[k, g] = jnp.broadcast_to(
                turned[g * HEADS : (g + 1) * HEADS, k : k + 1], (HEADS, CHUNK)
            )
    lead[...] = jnp.zeros_like(lead)
    state[...] = jnp.zeros_like(state)

    def lay_rows(target, c, g, first, end):
        for k in range(first, end):
            target[k * slab : k * slab + body, :] = recv[c, g * per_group + k].astype(F32)
            target[k * slab + body : (k + 1) * slab, :] = extra[
                g * per_group + k, pl.ds(c, 1), :
            ]

    def lay_out(c, g):
        lay_rows(rows, c, g, SPAN // slab, per_group)

    def lay_out_gates(c, g):
        lay_rows(gates, c, g, 0, -(-SPAN // slab))

    extras = extra_in.at[pl.ds(0, n - 1)]
    pltpu.make_async_copy(extras, extras, extra_recv).wait()

    def read_extra(device, _):
        extra[device] = extra_in[device].astype(F32)[:CHUNKS, :]
        return 0

    lax.fori_loop(0, n, read_extra, 0)
    blank = jnp.zeros((CHUNK - 3, CHUNK), F32)

    def read_past(g, _):
        for k in range(SPAN // slab, per_group):
            message = extra_in[g * per_group + k].astype(F32)
            first = jnp.transpose(jnp.concatenate([blank, message[8:11, :]], axis=0))
            second = jnp.transpose(jnp.concatenate([blank, message[11:14, :]], axis=0))
            rows[k * slab : k * slab + CHUNK, :] = first
            rows[k * slab + CHUNK : (k + 1) * slab, :] = second[: slab - CHUNK, :]
        for i in range(CONV // CHUNK):
            span = slice(i * CHUNK, (i + 1) * CHUNK)
            prev[g, span, :] = rows[SPAN + i * CHUNK : SPAN + (i + 1) * CHUNK, :]
        return 0

    lax.fori_loop(0, GROUPS, read_past, 0)

    def advance(u, _):
        c = u // GROUPS
        g = lax.rem(u, GROUPS)
        slot = lax.rem(u, HELD)

        @pl.when(g == 0)
        def _():
            wait_chunk(c)

            @pl.when(c + 1 + AHEAD < CHUNKS)
            def _():
                send_chunk(c + 1 + AHEAD, 0)

        lay_out(c, g)
        for i in range(CONV // CHUNK):
            span = slice(i * CHUNK, (i + 1) * CHUNK)
            current = rows[SPAN + i * CHUNK : SPAN + (i + 1) * CHUNK, :]
            past = prev[g, span, :]
            total = taps[g, 3, span, :] * current
            for k in range(1, 4):
                shifted = pltpu.roll(jnp.where(lane >= CHUNK - k, past, current), k, 1)
                total += taps[g, 3 - k, span, :] * shifted
            prev[g, span, :] = current
            value = silu(total)
            if i < SPAN // CHUNK:
                act[slot, span, :] = value.astype(BF16)
            elif i == SPAN // CHUNK:
                into[slot] = jnp.transpose(value).astype(BF16)
            else:
                outmap[slot] = value.astype(BF16)
                outrows[u] = jnp.transpose(value).astype(BF16)

        raw = rows[SPAN + CONV : COLS, :] + params[0, g]
        step = jnp.maximum(raw, 0.0) + jnp.log1p(jnp.exp(-jnp.abs(raw)))
        log_decay = -jnp.exp(params[1, g]) * step
        running = dot(log_decay, causal.astype(F32), lax.Precision.HIGHEST)
        last = jnp.broadcast_to(running[:, CHUNK - 1 :], (HEADS, CHUNK))
        until = jnp.exp(last - running) * step
        fade = jnp.exp(last)
        small[slot, 0] = running
        small[slot, 1] = jnp.exp(running)
        small[slot, 2] = jnp.exp(running + lead[g])
        lead[g] += last
        within[slot] = jnp.transpose(
            jnp.concatenate(
                [running - jnp.log(step), jnp.zeros((CHUNK - HEADS, CHUNK), F32)], axis=0
            )
        )
        cmat = outmap[slot]
        high = state[g].astype(BF16)
        low = (state[g] - high.astype(F32)).astype(BF16)
        carried[slot] = dot(
            jnp.concatenate([high, low], axis=1), jnp.concatenate([cmat, cmat], axis=0)
        )
        for h in range(HEADS):
            span = slice(h * HEAD_DIM, (h + 1) * HEAD_DIM)
            wgt[span, :] = (act[slot, span, :].astype(F32) * until[h : h + 1, :]).astype(BF16)
        update = dot(wgt[...], into[slot])
        for h in range(HEADS):
            span = slice(h * HEAD_DIM, (h + 1) * HEAD_DIM)
            state[g, span, :] = state[g, span, :] * fade[h : h + 1, :] + update[span, :]
        return 0

    def mix(u, _):
        c = u // GROUPS
        g = lax.rem(u, GROUPS)
        slot = lax.rem(u, HELD)
        lay_out_gates(c, g)
        scores = dot(into[slot], outmap[slot])
        columns = within[slot]
        for pair in range(HEADS // 2):
            owns = []
            reaches = []
            for h in (2 * pair, 2 * pair + 1):
                span = slice(h * HEAD_DIM, (h + 1) * HEAD_DIM)
                gaps = small[slot, 0, h : h + 1, :] - columns[:, h : h + 1]
                weights = (scores * jnp.exp(jnp.where(causal, gaps, -jnp.inf))).astype(BF16)
                x = act[slot, span, :]
                mixed = (
                    dot(x, weights)
                    + params[2, g, h : h + 1, :] * x.astype(F32)
                    + carried[slot, span, :] * small[slot, 1, h : h + 1, :]
                )
                gate = silu(gates[span, :])
                owns.append(mixed * gate)
                reaches.append(gate * small[slot, 2, h : h + 1, :])
            span = slice(pair * 2 * HEAD_DIM, (pair + 1) * 2 * HEAD_DIM)
            turned_own[u, :, span] = jnp.transpose(jnp.concatenate(owns, axis=0))
            turned_gate[u, :, span] = jnp.transpose(jnp.concatenate(reaches, axis=0))
        return 0

    def unit(u, _):
        advance(u, 0)
        mix(u, 0)
        return 0

    units = CHUNKS * GROUPS
    lax.fori_loop(0, units - HELD, unit, 0)

    low_sub = lax.broadcasted_iota(jnp.int32, (16, CHUNK), 0)

    def head_at(ref, position, height):
        return ref.at[pl.ds(pl.multiple_of(position * height, height), height)]

    def wait_messages(ref, count, height, sem):
        messages = ref.at[pl.ds(0, count * height)]
        pltpu.make_async_copy(messages, messages, sem).wait()

    mine = lax.rem(me, GROUPS)
    for g in range(GROUPS):
        advance(units - HELD + g, 0)
        for h in range(HEADS):
            first = (h * GROUPS + g) * MESSAGE
            own[first : first + HEAD_DIM, :] = state[
                g, h * HEAD_DIM : (h + 1) * HEAD_DIM, :
            ].astype(BF16)
            fade = jnp.broadcast_to(jnp.exp(lead[g, h : h + 1, :]), (16, CHUNK))
            high = fade.astype(BF16).astype(F32)
            middle = (fade - high).astype(BF16).astype(F32)
            parts = jnp.where(
                low_sub == 0,
                high,
                jnp.where(
                    low_sub == 1, middle, jnp.where(low_sub == 2, fade - high - middle, 0.0)
                ),
            )
            own[first + HEAD_DIM : first + MESSAGE, :] = parts.astype(BF16)

        def send_state(i, _):
            move = lax.rem(i * 5 + 6, HEADS)
            y = lax.rem(me // 8 + move // 4, 4)
            x = lax.rem(me // 2 + move, 4)
            device = y * 8 + x * 2 + g

            @pl.when(device != me)
            def _():
                pltpu.make_async_remote_copy(
                    src_ref=head_at(own, device, MESSAGE),
                    dst_ref=head_at(gathered, me, MESSAGE),
                    send_sem=scan_send,
                    recv_sem=scan_recv,
                    device_id={"seq": device},
                    device_id_type=MESH,
                ).start()

            return 0

        lax.fori_loop(0, HEADS, send_state, 0)
    head_at(gathered, me, MESSAGE)[...] = head_at(own, me, MESSAGE)[...]

    @pl.when(mine == 1)
    def _():
        lax.fori_loop(units - HELD, units, mix, 0)

    wait_messages(gathered, n - 1, MESSAGE, scan_recv)

    def horner(device, reached):
        head_at(prefix, device, HEAD_DIM)[...] = reached.astype(BF16)
        message = head_at(gathered, device, MESSAGE)[...].astype(F32)
        fade = jnp.sum(message[HEAD_DIM:, :], axis=0, keepdims=True)
        return reached * fade + message[:HEAD_DIM, :]

    lax.fori_loop(0, n, horner, jnp.zeros((HEAD_DIM, STATE_WIDTH), F32))
    slot = mine * HEADS + me // GROUPS

    def send_back(i, _):
        device = peer(i, 0)
        pltpu.make_async_remote_copy(
            src_ref=head_at(prefix, device, HEAD_DIM),
            dst_ref=head_at(incoming, slot, HEAD_DIM),
            send_sem=back_send,
            recv_sem=back_recv.at[mine],
            device_id={"seq": device},
            device_id_type=MESH,
        ).start()
        return 0

    lax.fori_loop(0, n - 1, send_back, 0)
    head_at(incoming, slot, HEAD_DIM)[...] = head_at(prefix, me, HEAD_DIM)[...]

    @pl.when(mine == 0)
    def _():
        lax.fori_loop(units - HELD, units, mix, 0)

    for g in range(GROUPS):

        @pl.when(mine == g)
        def _():
            wait_messages(incoming, HEADS - 1, HEAD_DIM, back_recv.at[g])

        @pl.when(mine != g)
        def _():
            wait_messages(incoming, HEADS, HEAD_DIM, back_recv.at[g])

        for i in range(SPAN // CHUNK):
            block = incoming[g * SPAN + i * CHUNK : g * SPAN + (i + 1) * CHUNK, :]
            turned_in[:, i * CHUNK : (i + 1) * CHUNK] = jnp.transpose(block.astype(F32)).astype(
                BF16
            )
        first = 1 + g * (SPAN // CHUNK)
        gain = jnp.concatenate(
            [pack_ref[first + i : first + i + 1, :] for i in range(SPAN // CHUNK)], axis=1
        )

        def finish(c, _):
            u = c * GROUPS + g
            arrived = dot(outrows[u], turned_in[...])
            for i in range(CHUNK // 16):
                span = slice(i * 16, (i + 1) * 16)
                gated = turned_own[u, span, :] + arrived[span, :] * turned_gate[u, span, :]
                squares = jnp.sum(gated * gated, axis=1, keepdims=True)
                scale = lax.rsqrt(squares * (1.0 / SPAN) + EPSILON)
                staged[u, span, :] = (gated * scale * gain).astype(BF16)
            pltpu.make_async_copy(
                staged.at[u],
                out_ref.at[
                    pl.ds(pl.multiple_of(c * CHUNK, CHUNK), CHUNK),
                    pl.ds(g * SPAN, SPAN),
                ],
                out_sem,
            ).start()
            return 0

        lax.fori_loop(0, CHUNKS, finish, 0)

    def drain(c, _):
        peers = recv.at[c, pl.ds(0, n - 1)]
        pltpu.make_async_copy(peers, peers, chunk_send.at[c]).wait()
        return 0

    lax.fori_loop(0, CHUNKS, drain, 0)
    pltpu.make_async_copy(extras, extras, extra_send).wait()
    wait_messages(own, n - 1, MESSAGE, scan_send)
    wait_messages(prefix, n - 1, HEAD_DIM, back_send)
    pltpu.make_async_copy(staged, staged, out_sem).wait()


def per_device(projected, conv_weight, dt_bias, a_log, d_skip, norm_gain):
    n = lax.axis_size("seq")
    slab = COLS * GROUPS // n
    tokens = CHUNK * CHUNKS
    units = GROUPS * CHUNKS
    heads = GROUPS * HEADS
    packed = jnp.concatenate(
        [dt_bias, a_log, d_skip, jnp.zeros((heads,), F32), norm_gain]
    ).reshape(-1, CHUNK)
    hbm = pl.BlockSpec(memory_space=pltpu.HBM)
    anywhere = pl.BlockSpec(memory_space=pl.ANY)
    dma = pltpu.SemaphoreType.DMA
    return pl.pallas_call(
        functools.partial(kernel, n),
        out_shape=jax.ShapeDtypeStruct((tokens, GROUPS * SPAN), BF16),
        in_specs=[hbm] * 3,
        out_specs=anywhere,
        scratch_shapes=[
            pltpu.VMEM((4, GROUPS, CONV), F32),
            pltpu.VMEM(packed.shape, F32),
            pltpu.VMEM((CHUNKS, n, slab - 1, CHUNK), BF16),
            pltpu.VMEM((COLS, CHUNK), F32),
            pltpu.VMEM((-(-SPAN // slab) * slab, CHUNK), F32),
            pltpu.VMEM((GROUPS, 4, CONV, CHUNK), F32),
            pltpu.VMEM((3, GROUPS, HEADS, CHUNK), F32),
            pltpu.VMEM((GROUPS, CONV, CHUNK), F32),
            pltpu.VMEM((HELD, SPAN, CHUNK), BF16),
            pltpu.VMEM((SPAN, CHUNK), BF16),
            pltpu.VMEM((GROUPS, SPAN, STATE_WIDTH), F32),
            pltpu.VMEM((HELD, SPAN, CHUNK), F32),
            pltpu.VMEM((HELD, CHUNK, CHUNK), F32),
            pltpu.VMEM((HELD, CHUNK, STATE_WIDTH), BF16),
            pltpu.VMEM((HELD, STATE_WIDTH, CHUNK), BF16),
            pltpu.VMEM((units, CHUNK, STATE_WIDTH), BF16),
            pltpu.VMEM((HELD, 3, HEADS, CHUNK), F32),
            pltpu.VMEM((GROUPS, HEADS, CHUNK), F32),
            pltpu.VMEM((units, CHUNK, SPAN), F32),
            pltpu.VMEM((units, CHUNK, SPAN), F32),
            pltpu.VMEM((n, slab, CHUNK), BF16),
            pltpu.VMEM((1, n * tokens), BF16),
            pltpu.VMEM((n, 16, CHUNK), BF16),
            pltpu.VMEM((n, 16, CHUNK), BF16),
            pltpu.VMEM((n, CHUNKS, CHUNK), F32),
            pltpu.VMEM((heads * MESSAGE, STATE_WIDTH), BF16),
            pltpu.VMEM((heads * MESSAGE, STATE_WIDTH), BF16),
            pltpu.VMEM((heads * HEAD_DIM, STATE_WIDTH), BF16),
            pltpu.VMEM((heads * HEAD_DIM, STATE_WIDTH), BF16),
            pltpu.VMEM((STATE_WIDTH, SPAN), BF16),
            pltpu.VMEM((units, CHUNK, SPAN), BF16),
            dma((CHUNKS,)), dma((CHUNKS,)), dma((CHUNKS,)), dma, dma, dma, dma,
            dma, dma, dma, dma((GROUPS,)), dma, dma((2,)),
        ],
        compiler_params=pltpu.CompilerParams(
            collective_id=0, has_side_effects=True, vmem_limit_bytes=48 * 2**20
        ),
    )(
        projected, conv_weight, packed
    )


def solution(mesh):
    in_specs = (P(("tp", "seq"), None), P(None, "tp", None), P("tp"), P("tp"), P("tp"), P("tp"))
    return jax.shard_map(
        per_device, mesh=mesh, in_specs=in_specs, out_specs=P("seq", "tp"), check_vma=False
    )
```

```python
import functools

import jax
import jax.numpy as jnp
from jax import lax
from jax.experimental import pallas as pl
from jax.experimental.pallas import tpu as pltpu
from jax.sharding import PartitionSpec as P

MESH = pl.DeviceIdType.MESH
HEAD_DIM = 64
STATE_WIDTH = 128
CHUNK = 128
CHUNKS = 8
GROUPS = 2
HEADS = 16
SPAN = HEADS * HEAD_DIM
CONV = SPAN + 2 * STATE_WIDTH
COLS = SPAN + CONV + HEADS
EPSILON = 1e-05
AHEAD = 3
HELD = 2
MESSAGE = HEAD_DIM + 16

F32 = jnp.float32
BF16 = jnp.bfloat16


def silu(v):
    return v * (1.0 / (1.0 + jnp.exp(-v)))


def dot(a, b, precision=None):
    return jnp.dot(a, b, preferred_element_type=F32, precision=precision)


def kernel(
    n, x_ref, conv_hbm, pack_hbm, out_ref,
    conv_ref, pack_ref, recv, rows, gates, taps, params, prev, act, wgt, state, carried, within, into,
    outmap, outrows, small, lead, turned_gate, turned_own,
    tails, spare, extra_out, extra_in, extra, own, gathered, prefix, incoming, turned_in, staged,
    chunk_send, chunk_recv, chunk_own, extra_send, extra_recv, tail_sem, spare_sem,
    scan_send, scan_recv, back_send, back_recv, out_sem, small_sem,
):
    me = lax.axis_index("seq")
    slab = COLS * GROUPS // n
    body = slab - 1
    per_group = n // GROUPS

    loads = (
        pltpu.make_async_copy(pack_hbm, pack_ref, small_sem.at[0]),
        pltpu.make_async_copy(conv_hbm, conv_ref, small_sem.at[1]),
    )
    for load in loads:
        load.start()
    spare_load = pltpu.make_async_copy(x_ref.at[pl.ds(body, 1), :], spare, spare_sem)
    spare_load.start()

    def load_tail(device, _):
        first = pl.multiple_of((device + 1) * CHUNK * CHUNKS - CHUNK, CHUNK)
        pltpu.make_async_copy(
            x_ref.at[:, pl.ds(first, CHUNK)], tails.at[device], tail_sem
        ).start()
        return 0

    lax.fori_loop(0, n, load_tail, 0)

    barrier = pltpu.get_barrier_semaphore()

    def greet(i, _):
        pl.semaphore_signal(
            barrier, inc=1, device_id={"seq": lax.rem(me + i, n)}, device_id_type=MESH
        )
        return 0

    lax.fori_loop(1, n, greet, 0)
    pl.semaphore_wait(barrier, n - 1)

    def peer(i, shift):
        move = lax.rem(i * 17 + shift, n - 1) + 1
        if n != 32:
            return lax.rem(me + move, n)
        y = lax.rem(me // 8 + move // 8, 4)
        x = lax.rem(me // 2 + move // 2, 4)
        core = lax.rem(me + move, 2)
        return y * 8 + x * 2 + core

    def piece(device, c):
        first = pl.multiple_of(device * (CHUNK * CHUNKS) + c * CHUNK, CHUNK)
        return x_ref.at[pl.ds(0, body), pl.ds(first, CHUNK)]

    def send_chunk(c, _):

        def send(i, _):
            device = peer(i, c * 2)
            pltpu.make_async_remote_copy(
                src_ref=piece(device, c),
                dst_ref=recv.at[c, me],
                send_sem=chunk_send.at[c],
                recv_sem=chunk_recv.at[c],
                device_id={"seq": device},
                device_id_type=MESH,
            ).start()
            return 0

        lax.fori_loop(0, n - 1, send, 0)
        pltpu.make_async_copy(piece(me, c), recv.at[c, me], chunk_own.at[c]).start()
        return 0

    send_chunk(0, 0)
    pltpu.make_async_copy(tails, tails, tail_sem).wait()
    spare_load.wait()

    def make_extra(device, _):
        before = lax.rem(device + n - 1, n)
        has_past = jnp.where(device > 0, 1.0, 0.0).astype(F32)
        tail = tails[before].astype(F32) * has_past
        first = jnp.transpose(tail[:CHUNK, :])
        second = jnp.transpose(
            jnp.concatenate([tail[CHUNK:, :], jnp.zeros((2 * CHUNK - slab, CHUNK), F32)], axis=0)
        )
        held = [
            spare[
                :, pl.ds(pl.multiple_of(device * (CHUNK * CHUNKS) + c * CHUNK, CHUNK), CHUNK)
            ].astype(F32)
            for c in range(CHUNKS)
        ]
        extra_out[device] = jnp.concatenate(
            held + [first[CHUNK - 3 :, :], second[CHUNK - 3 :, :], jnp.zeros((2, CHUNK), F32)],
            axis=0,
        ).astype(BF16)
        return 0

    lax.fori_loop(0, n, make_extra, 0)

    def send_extra(i, _):
        device = peer(i, 0)
        pltpu.make_async_remote_copy(
            src_ref=extra_out.at[device],
            dst_ref=extra_in.at[me],
            send_sem=extra_send,
            recv_sem=extra_recv,
            device_id={"seq": device},
            device_id_type=MESH,
        ).start()
        return 0

    lax.fori_loop(0, n - 1, send_extra, 0)
    extra_in[me] = extra_out[me]
    lax.fori_loop(1, AHEAD + 1, send_chunk, 0)

    def wait_chunk(c):
        peers = recv.at[c, pl.ds(0, n - 1)]
        pltpu.make_async_copy(peers, peers, chunk_recv.at[c]).wait()
        pltpu.make_async_copy(recv.at[c, 0], recv.at[c, 0], chunk_own.at[c]).wait()

    sub = lax.broadcasted_iota(jnp.int32, (CHUNK, CHUNK), 0)
    lane = lax.broadcasted_iota(jnp.int32, (CHUNK, CHUNK), 1)
    causal = sub <= lane

    for load in loads:
        load.wait()

    def taps_of(g, i):
        four = jnp.concatenate(
            [
                conv_ref[k, g : g + 1, i * CHUNK : (i + 1) * CHUNK]
                for k in range(4)
            ]
            + [jnp.zeros((CHUNK - 4, CHUNK), F32)],
            axis=0,
        )
        turned = jnp.transpose(four)
        for k in range(4):
            taps[g, k, i * CHUNK : (i + 1) * CHUNK, :] = jnp.broadcast_to(
                turned[:, k : k + 1], (CHUNK, CHUNK)
            )

    for g in range(GROUPS):
        for i in range(CONV // CHUNK):
            taps_of(g, i)
    rows[0:CHUNK, :] = jnp.zeros((CHUNK, CHUNK), F32)
    for k in range(3):
        rows[k : k + 1, 0 : GROUPS * HEADS] = pack_ref[
            0:1, k * GROUPS * HEADS : (k + 1) * GROUPS * HEADS
        ]
    turned = jnp.transpose(rows[0:CHUNK, :])
    for k in range(3):
        for g in range(GROUPS):
            params[k, g] = jnp.broadcast_to(
                turned[g * HEADS : (g + 1) * HEADS, k : k + 1], (HEADS, CHUNK)
            )
    lead[...] = jnp.zeros_like(lead)
    state[...] = jnp.zeros_like(state)

    def lay_rows(target, c, g, first, end):
        for k in range(first, end):
            target[k * slab : k * slab + body, :] = recv[c, g * per_group + k].astype(F32)
            target[k * slab + body : (k + 1) * slab, :] = extra[
                g * per_group + k, pl.ds(c, 1), :
            ]

    def lay_out(c, g):
        lay_rows(rows, c, g, SPAN // slab, per_group)

    def lay_out_gates(c, g):
        lay_rows(gates, c, g, 0, -(-SPAN // slab))

    extras = extra_in.at[pl.ds(0, n - 1)]
    pltpu.make_async_copy(extras, extras, extra_recv).wait()

    def read_extra(device, _):
        extra[device] = extra_in[device].astype(F32)[:CHUNKS, :]
        return 0

    lax.fori_loop(0, n, read_extra, 0)
    blank = jnp.zeros((CHUNK - 3, CHUNK), F32)

    def read_past(g, _):
        for k in range(SPAN // slab, per_group):
            message = extra_in[g * per_group + k].astype(F32)
            first = jnp.transpose(jnp.concatenate([blank, message[8:11, :]], axis=0))
            second = jnp.transpose(jnp.concatenate([blank, message[11:14, :]], axis=0))
            rows[k * slab : k * slab + CHUNK, :] = first
            rows[k * slab + CHUNK : (k + 1) * slab, :] = second[: slab - CHUNK, :]
        for i in range(CONV // CHUNK):
            span = slice(i * CHUNK, (i + 1) * CHUNK)
            prev[g, span, :] = rows[SPAN + i * CHUNK : SPAN + (i + 1) * CHUNK, :]
        return 0

    lax.fori_loop(0, GROUPS, read_past, 0)

    def advance(u, _):
        c = u // GROUPS
        g = lax.rem(u, GROUPS)
        slot = lax.rem(u, HELD)

        @pl.when(g == 0)
        def _():
            wait_chunk(c)

            @pl.when(c + 1 + AHEAD < CHUNKS)
            def _():
                send_chunk(c + 1 + AHEAD, 0)

        lay_out(c, g)
        for i in range(CONV // CHUNK):
            span = slice(i * CHUNK, (i + 1) * CHUNK)
            current = rows[SPAN + i * CHUNK : SPAN + (i + 1) * CHUNK, :]
            past = prev[g, span, :]
            total = taps[g, 3, span, :] * current
            for k in range(1, 4):
                shifted = pltpu.roll(jnp.where(lane >= CHUNK - k, past, current), k, 1)
                total += taps[g, 3 - k, span, :] * shifted
            prev[g, span, :] = current
            value = silu(total)
            if i < SPAN // CHUNK:
                act[slot, span, :] = value.astype(BF16)
            elif i == SPAN // CHUNK:
                into[slot] = jnp.transpose(value).astype(BF16)
            else:
                outmap[slot] = value.astype(BF16)
                outrows[u] = jnp.transpose(value).astype(BF16)

        raw = rows[SPAN + CONV : COLS, :] + params[0, g]
        step = jnp.maximum(raw, 0.0) + jnp.log1p(jnp.exp(-jnp.abs(raw)))
        log_decay = -jnp.exp(params[1, g]) * step
        running = dot(log_decay, causal.astype(F32), lax.Precision.HIGHEST)
        last = jnp.broadcast_to(running[:, CHUNK - 1 :], (HEADS, CHUNK))
        until = jnp.exp(last - running) * step
        fade = jnp.exp(last)
        small[slot, 0] = running
        small[slot, 1] = jnp.exp(running)
        small[slot, 2] = jnp.exp(running + lead[g])
        lead[g] += last
        within[slot] = jnp.transpose(
            jnp.concatenate(
                [running - jnp.log(step), jnp.zeros((CHUNK - HEADS, CHUNK), F32)], axis=0
            )
        )
        cmat = outmap[slot]
        high = state[g].astype(BF16)
        low = (state[g] - high.astype(F32)).astype(BF16)
        carried[slot] = dot(
            jnp.concatenate([high, low], axis=1), jnp.concatenate([cmat, cmat], axis=0)
        )
        for h in range(HEADS):
            span = slice(h * HEAD_DIM, (h + 1) * HEAD_DIM)
            wgt[span, :] = (act[slot, span, :].astype(F32) * until[h : h + 1, :]).astype(BF16)
        update = dot(wgt[...], into[slot])
        for h in range(HEADS):
            span = slice(h * HEAD_DIM, (h + 1) * HEAD_DIM)
            state[g, span, :] = state[g, span, :] * fade[h : h + 1, :] + update[span, :]
        return 0

    def mix(u, _):
        c = u // GROUPS
        g = lax.rem(u, GROUPS)
        slot = lax.rem(u, HELD)
        lay_out_gates(c, g)
        scores = dot(into[slot], outmap[slot])
        columns = within[slot]
        for pair in range(HEADS // 2):
            owns = []
            reaches = []
            for h in (2 * pair, 2 * pair + 1):
                span = slice(h * HEAD_DIM, (h + 1) * HEAD_DIM)
                gaps = small[slot, 0, h : h + 1, :] - columns[:, h : h + 1]
                weights = (scores * jnp.exp(jnp.where(causal, gaps, -jnp.inf))).astype(BF16)
                x = act[slot, span, :]
                mixed = (
                    dot(x, weights)
                    + params[2, g, h : h + 1, :] * x.astype(F32)
                    + carried[slot, span, :] * small[slot, 1, h : h + 1, :]
                )
                gate = silu(gates[span, :])
                owns.append(mixed * gate)
                reaches.append(gate * small[slot, 2, h : h + 1, :])
            span = slice(pair * 2 * HEAD_DIM, (pair + 1) * 2 * HEAD_DIM)
            turned_own[u, :, span] = jnp.transpose(jnp.concatenate(owns, axis=0))
            turned_gate[u, :, span] = jnp.transpose(jnp.concatenate(reaches, axis=0))
        return 0

    def unit(u, _):
        advance(u, 0)
        mix(u, 0)
        return 0

    units = CHUNKS * GROUPS
    lax.fori_loop(0, units - HELD, unit, 0)

    low_sub = lax.broadcasted_iota(jnp.int32, (16, CHUNK), 0)

    def head_at(ref, position, height):
        return ref.at[pl.ds(pl.multiple_of(position * height, height), height)]

    def wait_messages(ref, count, height, sem):
        messages = ref.at[pl.ds(0, count * height)]
        pltpu.make_async_copy(messages, messages, sem).wait()

    mine = lax.rem(me, GROUPS)
    for g in range(GROUPS):
        advance(units - HELD + g, 0)
        for h in range(HEADS):
            first = (h * GROUPS + g) * MESSAGE
            own[first : first + HEAD_DIM, :] = state[
                g, h * HEAD_DIM : (h + 1) * HEAD_DIM, :
            ].astype(BF16)
            fade = jnp.broadcast_to(jnp.exp(lead[g, h : h + 1, :]), (16, CHUNK))
            high = fade.astype(BF16).astype(F32)
            middle = (fade - high).astype(BF16).astype(F32)
            parts = jnp.where(
                low_sub == 0,
                high,
                jnp.where(
                    low_sub == 1, middle, jnp.where(low_sub == 2, fade - high - middle, 0.0)
                ),
            )
            own[first + HEAD_DIM : first + MESSAGE, :] = parts.astype(BF16)

        def send_state(i, _):
            move = lax.rem(i * 5 + 6, HEADS)
            y = lax.rem(me // 8 + move // 4, 4)
            x = lax.rem(me // 2 + move, 4)
            device = y * 8 + x * 2 + g

            @pl.when(device != me)
            def _():
                pltpu.make_async_remote_copy(
                    src_ref=head_at(own, device, MESSAGE),
                    dst_ref=head_at(gathered, me, MESSAGE),
                    send_sem=scan_send,
                    recv_sem=scan_recv,
                    device_id={"seq": device},
                    device_id_type=MESH,
                ).start()

            return 0

        lax.fori_loop(0, HEADS, send_state, 0, unroll=True)
    head_at(gathered, me, MESSAGE)[...] = head_at(own, me, MESSAGE)[...]

    @pl.when(mine == 1)
    def _():
        lax.fori_loop(units - HELD, units, mix, 0)

    wait_messages(gathered, n - 1, MESSAGE, scan_recv)

    def horner(device, reached):
        head_at(prefix, device, HEAD_DIM)[...] = reached.astype(BF16)
        message = head_at(gathered, device, MESSAGE)[...].astype(F32)
        fade = jnp.sum(message[HEAD_DIM:, :], axis=0, keepdims=True)
        return reached * fade + message[:HEAD_DIM, :]

    lax.fori_loop(0, n, horner, jnp.zeros((HEAD_DIM, STATE_WIDTH), F32), unroll=8)
    slot = mine * HEADS + me // GROUPS

    def send_back(i, _):
        device = peer(i, 0)
        pltpu.make_async_remote_copy(
            src_ref=head_at(prefix, device, HEAD_DIM),
            dst_ref=head_at(incoming, slot, HEAD_DIM),
            send_sem=back_send,
            recv_sem=back_recv.at[mine],
            device_id={"seq": device},
            device_id_type=MESH,
        ).start()
        return 0

    lax.fori_loop(0, n - 1, send_back, 0, unroll=True)
    head_at(incoming, slot, HEAD_DIM)[...] = head_at(prefix, me, HEAD_DIM)[...]

    @pl.when(mine == 0)
    def _():
        lax.fori_loop(units - HELD, units, mix, 0)

    for g in range(GROUPS):

        @pl.when(mine == g)
        def _():
            wait_messages(incoming, HEADS - 1, HEAD_DIM, back_recv.at[g])

        @pl.when(mine != g)
        def _():
            wait_messages(incoming, HEADS, HEAD_DIM, back_recv.at[g])

        for i in range(SPAN // CHUNK):
            block = incoming[g * SPAN + i * CHUNK : g * SPAN + (i + 1) * CHUNK, :]
            turned_in[:, i * CHUNK : (i + 1) * CHUNK] = jnp.transpose(block.astype(F32)).astype(
                BF16
            )
        first = 1 + g * (SPAN // CHUNK)
        gain = jnp.concatenate(
            [pack_ref[first + i : first + i + 1, :] for i in range(SPAN // CHUNK)], axis=1
        )

        def finish(c, _):
            u = c * GROUPS + g
            arrived = dot(outrows[u], turned_in[...])
            for i in range(CHUNK // 16):
                span = slice(i * 16, (i + 1) * 16)
                gated = turned_own[u, span, :] + arrived[span, :] * turned_gate[u, span, :]
                squares = jnp.sum(gated * gated, axis=1, keepdims=True)
                scale = lax.rsqrt(squares * (1.0 / SPAN) + EPSILON)
                staged[u, span, :] = (gated * scale * gain).astype(BF16)
            pltpu.make_async_copy(
                staged.at[u],
                out_ref.at[
                    pl.ds(pl.multiple_of(c * CHUNK, CHUNK), CHUNK),
                    pl.ds(g * SPAN, SPAN),
                ],
                out_sem,
            ).start()
            return 0

        lax.fori_loop(0, CHUNKS, finish, 0)

    def drain(c, _):
        peers = recv.at[c, pl.ds(0, n - 1)]
        pltpu.make_async_copy(peers, peers, chunk_send.at[c]).wait()
        return 0

    lax.fori_loop(0, CHUNKS, drain, 0)
    pltpu.make_async_copy(extras, extras, extra_send).wait()
    wait_messages(own, n - 1, MESSAGE, scan_send)
    wait_messages(prefix, n - 1, HEAD_DIM, back_send)
    pltpu.make_async_copy(staged, staged, out_sem).wait()


def per_device(projected, conv_weight, dt_bias, a_log, d_skip, norm_gain):
    n = lax.axis_size("seq")
    slab = COLS * GROUPS // n
    tokens = CHUNK * CHUNKS
    units = GROUPS * CHUNKS
    heads = GROUPS * HEADS
    packed = jnp.concatenate(
        [dt_bias, a_log, d_skip, jnp.zeros((heads,), F32), norm_gain]
    ).reshape(-1, CHUNK)
    hbm = pl.BlockSpec(memory_space=pltpu.HBM)
    anywhere = pl.BlockSpec(memory_space=pl.ANY)
    dma = pltpu.SemaphoreType.DMA
    return pl.pallas_call(
        functools.partial(kernel, n),
        out_shape=jax.ShapeDtypeStruct((tokens, GROUPS * SPAN), BF16),
        in_specs=[hbm] * 3,
        out_specs=anywhere,
        scratch_shapes=[
            pltpu.VMEM((4, GROUPS, CONV), F32),
            pltpu.VMEM(packed.shape, F32),
            pltpu.VMEM((CHUNKS, n, slab - 1, CHUNK), BF16),
            pltpu.VMEM((COLS, CHUNK), F32),
            pltpu.VMEM((-(-SPAN // slab) * slab, CHUNK), F32),
            pltpu.VMEM((GROUPS, 4, CONV, CHUNK), F32),
            pltpu.VMEM((3, GROUPS, HEADS, CHUNK), F32),
            pltpu.VMEM((GROUPS, CONV, CHUNK), F32),
            pltpu.VMEM((HELD, SPAN, CHUNK), BF16),
            pltpu.VMEM((SPAN, CHUNK), BF16),
            pltpu.VMEM((GROUPS, SPAN, STATE_WIDTH), F32),
            pltpu.VMEM((HELD, SPAN, CHUNK), F32),
            pltpu.VMEM((HELD, CHUNK, CHUNK), F32),
            pltpu.VMEM((HELD, CHUNK, STATE_WIDTH), BF16),
            pltpu.VMEM((HELD, STATE_WIDTH, CHUNK), BF16),
            pltpu.VMEM((units, CHUNK, STATE_WIDTH), BF16),
            pltpu.VMEM((HELD, 3, HEADS, CHUNK), F32),
            pltpu.VMEM((GROUPS, HEADS, CHUNK), F32),
            pltpu.VMEM((units, CHUNK, SPAN), F32),
            pltpu.VMEM((units, CHUNK, SPAN), F32),
            pltpu.VMEM((n, slab, CHUNK), BF16),
            pltpu.VMEM((1, n * tokens), BF16),
            pltpu.VMEM((n, 16, CHUNK), BF16),
            pltpu.VMEM((n, 16, CHUNK), BF16),
            pltpu.VMEM((n, CHUNKS, CHUNK), F32),
            pltpu.VMEM((heads * MESSAGE, STATE_WIDTH), BF16),
            pltpu.VMEM((heads * MESSAGE, STATE_WIDTH), BF16),
            pltpu.VMEM((heads * HEAD_DIM, STATE_WIDTH), BF16),
            pltpu.VMEM((heads * HEAD_DIM, STATE_WIDTH), BF16),
            pltpu.VMEM((STATE_WIDTH, SPAN), BF16),
            pltpu.VMEM((units, CHUNK, SPAN), BF16),
            dma((CHUNKS,)), dma((CHUNKS,)), dma((CHUNKS,)), dma, dma, dma, dma,
            dma, dma, dma, dma((GROUPS,)), dma, dma((2,)),
        ],
        compiler_params=pltpu.CompilerParams(
            collective_id=0, has_side_effects=True, vmem_limit_bytes=48 * 2**20
        ),
    )(
        projected, conv_weight, packed
    )


def solution(mesh):
    in_specs = (P(("tp", "seq"), None), P(None, "tp", None), P("tp"), P("tp"), P("tp"), P("tp"))
    return jax.shard_map(
        per_device, mesh=mesh, in_specs=in_specs, out_specs=P("seq", "tp"), check_vma=False
    )
```
